128 devices in a mesh: seq: 32 (over y, z, core), head: 4 (over x).
Axes of the slice: x: 4, y: 4, z: 4, core: 2. Of those that a mesh axis runs over, the one named last changes fastest.
Arguments:
- queries: bfloat16 [24576, 64, 128], P('seq', 'head'), may hold values from -6 to 6
- keys: bfloat16 [24576, 64, 128], P('seq', 'head'), may hold values from -6 to 6
- values: bfloat16 [24576, 64, 128], P('seq', 'head'), may hold values from -6 to 6
- out_grad: bfloat16 [24576, 64, 128], P('seq', 'head'), may hold values from -8 to 8
- gain: float32 [64, 128], P('head'), may hold values from 0.1 to 1.9
- entry_state: float32 [64, 128, 128], P('head'), may hold values from -3547.24 to 3547.24
Outputs:
- normed: bfloat16 [24576, 64, 128], P('seq', 'head')
- query_grad: bfloat16 [24576, 64, 128], P('seq', 'head')
- key_grad: bfloat16 [24576, 64, 128], P('seq', 'head')
- value_grad: bfloat16 [24576, 64, 128], P('seq', 'head')
- entry_grad: float32 [64, 128, 128], P('head', 'seq')
The draws below stay inside these ranges and needn't reach their ends.
All inputs are finite; a program needn't handle non-finite values.
Results may differ from the reference program's by a relative error of at most 0.006.
Values sent between devices are 32-bit elements; how exact they have to be, the bound alone decides.
No kernel may reach another device: no remote copies, remote signals or barrier semaphores. Data moves between devices by JAX's collectives and lax.ppermute only.
A program may use at most 256 MiB of HBM per device.

```python
import jax
import jax.numpy as jnp
from jax import lax

H = 64
E = 128
TOK_DEV = 768
TOKENS = 24576


def shared_scale(key):
    flipped = jax.random.bernoulli(jax.random.fold_in(key, 102), 0.5, (H, E))
    spread = jax.random.uniform(jax.random.fold_in(key, 103), (H, E), jnp.float32, 1.0, 2.0)
    return jnp.where(flipped, spread, -spread)


def flatten_law(normal_part):
    return normal_part


def shared_tokens(key):
    normal_part = jnp.clip(jax.random.normal(jax.random.fold_in(key, 101), (TOKENS, H, E), jnp.float32), -6.0, 6.0)
    return flatten_law(normal_part)


def draw_queries(key, part):
    common_part = shared_tokens(key)
    return common_part.astype(jnp.bfloat16)


def draw_out_grad(key, part):
    common_part = shared_tokens(key)
    signed_scale = shared_scale(key)
    key = jax.random.fold_in(key, 2)
    own_noise = jnp.clip(jax.random.normal(key, (TOKENS, H, E), jnp.float32), -6.0, 6.0)
    own_noise = flatten_law(own_noise)
    mixed = 0.7 * own_noise + 0.7 * (signed_scale / 1.5) * common_part
    return jnp.clip(mixed, -8.0, 8.0).astype(jnp.bfloat16)


def draw_entry_state(key, part):
    signed_scale = shared_scale(key)
    key = jax.random.fold_in(key, 3)
    strength = float(E * TOKENS) ** 0.5
    off_noise = jnp.clip(jax.random.normal(key, (H, E, E), jnp.float32), -6.0, 6.0)
    off_part = flatten_law(off_noise) * (0.5 * strength / float(E) ** 0.5)
    identity = jnp.eye(E, dtype=jnp.float32)[None]
    return off_part * (1.0 - identity) + strength * signed_scale[:, :, None] * identity


def block_levels(stream_key, dims, cuts, smallest, top_value):
    def one(axis_at, shards_of):
        steps = jax.random.uniform(jax.random.fold_in(jax.random.fold_in(stream_key, 6), axis_at), (shards_of,), jnp.float32, smallest / len(cuts), top_value / len(cuts))
        return jnp.repeat(jnp.exp(steps), dims[axis_at] // shards_of).reshape((-1,) + (1,) * (len(dims) - axis_at - 1))

    factor_of = one(*cuts[0])
    for cut in cuts[1:]:
        factor_of = factor_of * one(*cut)
    return factor_of


def gaussian(key, extent, scale, limit, cuts=(), kind=jnp.bfloat16):
    values = jax.random.normal(key, extent, jnp.float32) * scale
    if len(cuts) > 0:
        values = block_levels(key, extent, cuts, -0.22, 0.18) * values
    return jnp.clip(values, min=-limit, max=limit).astype(kind)


def setup_inputs(seed: int = 0) -> dict:
    arg_keys = jax.random.split(jax.random.key(seed), 7)
    queries = draw_queries(jax.random.fold_in(arg_keys[6], 71), 0)
    keys = gaussian(arg_keys[1], (TOKENS, H, E), 1.0, 6.0, ((0, 32), (1, 4)))
    values = gaussian(arg_keys[2], (TOKENS, H, E), 1.0, 6.0, ((0, 32), (1, 4)))
    out_grad = draw_out_grad(jax.random.fold_in(arg_keys[6], 71), 0)
    gain = jnp.clip(1.0 + 0.18 * jax.random.normal(arg_keys[4], (H, E), jnp.float32), 0.1, 1.9)
    entry_state = draw_entry_state(jax.random.fold_in(arg_keys[6], 71), 0)
    return dict(queries=queries, keys=keys, values=values, out_grad=out_grad, gain=gain, entry_state=entry_state)


epsilon = 1e-06

def to_bf(array):
    return lax.optimization_barrier(array.astype(jnp.bfloat16)).astype(jnp.float32)

def reference(queries, keys, values, out_grad, gain, entry_state):
    block_count = TOKENS // TOK_DEV

    def blocks(array):
        return array.reshape(block_count, TOK_DEV, H, E)
    row_index = jnp.arange(TOK_DEV)[:, None]
    col_index = jnp.arange(TOK_DEV)[None, :]
    causal = (col_index <= row_index)[None]
    gain_f32 = gain.astype(jnp.float32)
    total_width = H * E

    def forward(state, block_in):
        query_f, key_f, value_f, grad_f = (x.astype(jnp.float32) for x in block_in)
        state_bf = to_bf(state)
        causal_qk = to_bf(jnp.where(causal, jnp.einsum('thj,shj->hts', query_f, key_f), 0.0))
        attended = jnp.einsum('thj,hje->the', query_f, state_bf) + jnp.einsum('hts,she->the', causal_qk, value_f)
        sq_sum = lax.optimization_barrier(jnp.sum(attended * attended, axis=(1, 2)))
        rms_value = jnp.sqrt(sq_sum / total_width + epsilon)[:, None, None]
        normed = (gain_f32 * attended / rms_value).astype(jnp.bfloat16)
        upstream = gain_f32 * grad_f
        inner_sum = lax.optimization_barrier(jnp.sum(upstream * attended, axis=(1, 2)))[:, None, None]
        pre_grad = (upstream - attended * inner_sum / (total_width * rms_value * rms_value)) / rms_value
        pre_bf = pre_grad.astype(jnp.bfloat16)
        pre_f = to_bf(pre_grad)
        causal_gv = to_bf(jnp.where(causal, jnp.einsum('the,she->hts', pre_f, value_f), 0.0))
        query_grad = (jnp.einsum('the,hje->thj', pre_f, state_bf) + jnp.einsum('hts,shj->thj', causal_gv, key_f)).astype(jnp.bfloat16)
        next_state = state + jnp.einsum('thj,the->hje', key_f, value_f)
        return (next_state, (normed, query_grad, pre_bf))
    _, (normed, query_grad, pre_saved) = lax.scan(forward, entry_state.astype(jnp.float32), (blocks(queries), blocks(keys), blocks(values), blocks(out_grad)))

    def backward(suffix, block_in):
        query_f, key_f, value_f, pre_f = (x.astype(jnp.float32) for x in block_in)
        later_bf = to_bf(suffix)
        causal_qk = to_bf(jnp.where(causal, jnp.einsum('thj,shj->hts', query_f, key_f), 0.0))
        causal_gv = to_bf(jnp.where(causal, jnp.einsum('the,she->hts', pre_f, value_f), 0.0))
        key_grad = (jnp.einsum('the,hje->thj', value_f, later_bf) + jnp.einsum('hts,thj->shj', causal_gv, query_f)).astype(jnp.bfloat16)
        value_grad = (jnp.einsum('thj,hje->the', key_f, later_bf) + jnp.einsum('hts,the->she', causal_qk, pre_f)).astype(jnp.bfloat16)
        return (suffix + jnp.einsum('thj,the->hje', query_f, pre_f), (key_grad, value_grad))
    grand_total, (key_grad, value_grad) = lax.scan(backward, jnp.zeros((H, E, E), jnp.float32), (blocks(queries), blocks(keys), blocks(values), pre_saved), reverse=True)

    def whole(array):
        return array.reshape(TOKENS, H, E)
    return (whole(normed), whole(query_grad), whole(key_grad), whole(value_grad), grand_total)
```

```python
import jax
import jax.numpy as jnp
from jax import lax
from jax.experimental import pallas as pl
from jax.experimental.pallas import tpu as pltpu
from jax.sharding import PartitionSpec as P

H = 64
E = 128
T = 768
HL = 16
C = 256
NC = T // C
N = 32
WIDTH = H * E
epsilon = 1e-06
f32 = jnp.float32
bf16 = jnp.bfloat16
MIB = 1 << 20


def mm(a, b):
    return lax.dot_general(a, b, (((1,), (0,)), ((), ())), preferred_element_type=f32)


def mm_nt(a, b):
    return lax.dot_general(a, b, (((1,), (1,)), ((), ())), preferred_element_type=f32)


def mm_tn(a, b):
    return lax.dot_general(a, b, (((0,), (0,)), ((), ())), preferred_element_type=f32)


def causal():
    row = lax.broadcasted_iota(jnp.int32, (C, C), 0)
    col = lax.broadcasted_iota(jnp.int32, (C, C), 1)
    return col <= row


def heads_first(ref):
    return jnp.swapaxes(ref[...], 0, 1)


def params(vmem=40):
    return pltpu.CompilerParams(vmem_limit_bytes=vmem * MIB)


def tok_spec(order=None):
    return pl.BlockSpec((C, HL, E), order or (lambda i: (i, 0, 0)))


def head_spec(order=None):
    return pl.BlockSpec((HL, C, E), order or (lambda i: (0, i, 0)))


def whole(shape):
    return pl.BlockSpec(shape, lambda i: (0,) * len(shape))


def cost(flops, moved):
    return pl.CostEstimate(flops=flops, bytes_accessed=moved, transcendentals=0)


def kv_kernel(k_ref, v_ref, o_ref):
    @pl.when(pl.program_id(0) == 0)
    def _():
        o_ref[...] = jnp.zeros_like(o_ref)

    k = heads_first(k_ref)
    v = heads_first(v_ref)
    for h in range(HL):
        o_ref[h] += mm_tn(k[h], v[h])


def kv_sums(keys, values):
    return pl.pallas_call(
        kv_kernel,
        grid=(NC,),
        in_specs=[tok_spec(), tok_spec()],
        out_specs=whole((HL, E, E)),
        out_shape=jax.ShapeDtypeStruct((HL, E, E), f32),
        compiler_params=params(),
        cost_estimate=cost(2 * T * HL * E * E, 7 * MIB),
        name="kv_sums",
    )(keys, values)


def prefix_kernel(r_ref, x_ref, o_ref):
    total = x_ref[...]
    for i in range(N):
        o_ref[i] = total
        total = total + r_ref[i]


def prefix(pieces, start):
    return pl.pallas_call(
        prefix_kernel,
        out_shape=jax.ShapeDtypeStruct(pieces.shape, f32),
        compiler_params=params(8),
        cost_estimate=cost(N * 64 * E, 2 * MIB),
        name="prefix",
    )(pieces, start)


def suffix_kernel(r_ref, o_ref, t_ref):
    total = jnp.zeros_like(t_ref)
    for i in reversed(range(N)):
        o_ref[i] = total
        total = total + r_ref[i]
    t_ref[...] = total


def suffix(pieces):
    return pl.pallas_call(
        suffix_kernel,
        out_shape=[
            jax.ShapeDtypeStruct(pieces.shape, f32),
            jax.ShapeDtypeStruct(pieces.shape[1:], f32),
        ],
        compiler_params=params(8),
        cost_estimate=cost(N * 64 * E, 2 * MIB),
        name="suffix",
    )(pieces)


def local_kernel(q_ref, k_ref, v_ref, g_ref, qh_ref, kh_ref, vh_ref, gh_ref, att_ref, loc_ref, acc):
    @pl.when(pl.program_id(0) == 0)
    def _():
        acc[...] = jnp.zeros_like(acc)

    mask = causal()
    q = heads_first(q_ref)
    k = heads_first(k_ref)
    v = heads_first(v_ref)
    qh_ref[...] = q
    kh_ref[...] = k
    vh_ref[...] = v
    gh_ref[...] = heads_first(g_ref)
    for h in range(HL):
        qk = jnp.where(mask, mm_nt(q[h], k[h]), 0.0).astype(bf16)
        loc = acc[h].astype(bf16)
        loc_ref[0, h] = loc
        att_ref[h] = (mm(qk, v[h]) + mm(q[h], loc)).astype(bf16)
        acc[h] += mm_tn(k[h], v[h])


def local_part(queries, keys, values, out_grad):
    major = jax.ShapeDtypeStruct((HL, T, E), bf16)
    return pl.pallas_call(
        local_kernel,
        grid=(NC,),
        in_specs=[tok_spec()] * 4,
        out_specs=[head_spec()] * 5 + [pl.BlockSpec((1, HL, E, E), lambda i: (i, 0, 0, 0))],
        out_shape=[major] * 5 + [jax.ShapeDtypeStruct((NC, HL, E, E), bf16)],
        scratch_shapes=[pltpu.VMEM((HL, E, E), f32)],
        compiler_params=params(),
        cost_estimate=cost(2 * T * HL * (2 * C * E + 2 * E * E), 30 * MIB),
        name="local_part",
    )(queries, keys, values, out_grad)


def stats_kernel(q_ref, g_ref, a_ref, s_ref, gain_ref, o_ref):
    sq = jnp.zeros((C, E), f32)
    pr = jnp.zeros((C, E), f32)
    for h in range(HL):
        att = a_ref[h].astype(f32) + mm(q_ref[h], s_ref[h].astype(bf16))
        up = gain_ref[h : h + 1, :] * g_ref[h].astype(f32)
        sq = sq + att * att
        pr = pr + up * att
    o_ref[0:1, :] = jnp.sum(sq.T, axis=0, keepdims=True)
    o_ref[1:2, :] = jnp.sum(pr.T, axis=0, keepdims=True)


def stats(qh, gh, att, state, gain):
    return pl.pallas_call(
        stats_kernel,
        grid=(NC,),
        in_specs=[head_spec()] * 3 + [whole((HL, E, E)), whole((HL, E))],
        out_specs=pl.BlockSpec((2, C), lambda i: (0, i)),
        out_shape=jax.ShapeDtypeStruct((2, T), f32),
        compiler_params=params(),
        cost_estimate=cost(2 * T * HL * E * E, 10 * MIB),
        name="stats",
    )(qh, gh, att, state, gain)


def scales(sums):
    rms = jnp.sqrt(sums[0:1, :] / WIDTH + epsilon)
    a = 1.0 / rms
    b = sums[1:2, :] / (WIDTH * rms * rms) * a
    a = jnp.broadcast_to(a, (E, C)).T
    b = jnp.broadcast_to(b, (E, C)).T
    return a, b


def pre_kernel(q_ref, g_ref, a_ref, s_ref, gain_ref, sums_ref, p_ref, wl_ref, w_ref, acc):
    step = pl.program_id(0)

    @pl.when(step == 0)
    def _():
        acc[...] = jnp.zeros_like(acc)

    a, b = scales(sums_ref)
    for h in range(HL):
        q = q_ref[h]
        att = a_ref[h].astype(f32) + mm(q, s_ref[h].astype(bf16))
        up = gain_ref[h : h + 1, :] * g_ref[h].astype(f32)
        p = (up * a - att * b).astype(bf16)
        p_ref[h] = p
        wl_ref[0, h] = acc[h].astype(bf16)
        acc[h] += mm_tn(q, p)

    @pl.when(step == NC - 1)
    def _():
        low = lax.broadcasted_iota(jnp.int32, (HL, 8, E), 1) < 4
        for h in range(0, HL, 2):
            x = acc[h].reshape(HL, 8, E)
            y = acc[h + 1].reshape(HL, 8, E)
            w_ref[:, 0, 4 * h : 4 * h + 8, :] = jnp.where(low, x, pltpu.roll(y, 4, 1))
            w_ref[:, 1, 4 * h : 4 * h + 8, :] = jnp.where(low, pltpu.roll(x, 4, 1), y)


def pre_part(qh, gh, att, state, gain, sums):
    back = lambda i: (0, NC - 1 - i, 0)
    return pl.pallas_call(
        pre_kernel,
        grid=(NC,),
        in_specs=[head_spec(back)] * 3
        + [whole((HL, E, E)), whole((HL, E)), pl.BlockSpec((2, C), lambda i: (0, NC - 1 - i))],
        out_specs=[
            head_spec(back),
            pl.BlockSpec((1, HL, E, E), lambda i: (NC - 1 - i, 0, 0, 0)),
            whole((16, 2, 64, E)),
        ],
        out_shape=[
            jax.ShapeDtypeStruct((HL, T, E), bf16),
            jax.ShapeDtypeStruct((NC, HL, E, E), bf16),
            jax.ShapeDtypeStruct((16, 2, 64, E), f32),
        ],
        scratch_shapes=[pltpu.VMEM((HL, E, E), f32)],
        compiler_params=params(),
        cost_estimate=cost(4 * T * HL * E * E, 16 * MIB),
        name="pre_part",
    )(qh, gh, att, state, gain, sums)


def query_kernel(q_ref, k_ref, v_ref, p_ref, a_ref, s_ref, loc_ref, gain_ref, sums_ref, n_ref, qg_ref, gv_ref):
    mask = causal()
    a, _ = scales(sums_ref)
    normed = []
    grads = []
    for h in range(HL):
        state = s_ref[h].astype(bf16)
        att = a_ref[h].astype(f32) + mm(q_ref[h], state)
        normed.append((gain_ref[h : h + 1, :] * att * a).astype(bf16))
        p = p_ref[h]
        gv = jnp.where(mask, mm_nt(p, v_ref[h]), 0.0).astype(bf16)
        gv_ref[h] = gv
        grads.append((mm_nt(p, state) + mm_nt(p, loc_ref[0, h]) + mm(gv, k_ref[h])).astype(bf16))
    n_ref[...] = jnp.swapaxes(jnp.stack(normed), 0, 1)
    qg_ref[...] = jnp.swapaxes(jnp.stack(grads), 0, 1)


def query_part(qh, kh, vh, pre, att, state, loc, gain, sums):
    tok = jax.ShapeDtypeStruct((T, HL, E), bf16)
    return pl.pallas_call(
        query_kernel,
        grid=(NC,),
        in_specs=[head_spec()] * 5
        + [
            whole((HL, E, E)),
            pl.BlockSpec((1, HL, E, E), lambda i: (i, 0, 0, 0)),
            whole((HL, E)),
            pl.BlockSpec((2, C), lambda i: (0, i)),
        ],
        out_specs=[tok_spec()] * 2 + [pl.BlockSpec((HL, C, C), lambda i: (0, i, 0))],
        out_shape=[tok] * 2 + [jax.ShapeDtypeStruct((HL, T, C), bf16)],
        compiler_params=params(),
        cost_estimate=cost(2 * T * HL * (2 * C * E + 3 * E * E), 30 * MIB),
        name="query_part",
    )(qh, kh, vh, pre, att, state, loc, gain, sums)


def keyval_kernel(q_ref, k_ref, v_ref, p_ref, gv_ref, wl_ref, kg_ref, vg_ref):
    mask = causal()
    for h in range(HL):
        later = wl_ref[0, h]
        qk = jnp.where(mask, mm_nt(q_ref[h], k_ref[h]), 0.0).astype(bf16)
        kg_ref[h] = (mm_tn(gv_ref[h], q_ref[h]) + mm_nt(v_ref[h], later)).astype(bf16)
        vg_ref[h] = (mm_tn(qk, p_ref[h]) + mm(k_ref[h], later)).astype(bf16)


def keyval_part(qh, kh, vh, pre, gv, wloc):
    major = jax.ShapeDtypeStruct((HL, T, E), bf16)
    return pl.pallas_call(
        keyval_kernel,
        grid=(NC,),
        in_specs=[head_spec()] * 4
        + [
            pl.BlockSpec((HL, C, C), lambda i: (0, i, 0)),
            pl.BlockSpec((1, HL, E, E), lambda i: (i, 0, 0, 0)),
        ],
        out_specs=[head_spec()] * 2,
        out_shape=[major] * 2,
        compiler_params=params(),
        cost_estimate=cost(2 * T * HL * (3 * C * E + 2 * E * E), 28 * MIB),
        name="keyval_part",
    )(qh, kh, vh, pre, gv, wloc)


def final_kernel(k_ref, v_ref, kp_ref, vp_ref, l_ref, kg_ref, vg_ref):
    low = lax.broadcasted_iota(jnp.int32, (HL, 8, E), 1) < 4
    kg = []
    vg = []
    for h in range(0, HL, 2):
        even = l_ref[:, 0, 4 * h : 4 * h + 8, :]
        odd = l_ref[:, 1, 4 * h : 4 * h + 8, :]
        first = jnp.where(low, even, pltpu.roll(odd, 4, 1)).reshape(E, E).astype(bf16)
        second = jnp.where(low, pltpu.roll(even, 4, 1), odd).reshape(E, E).astype(bf16)
        for at, later in ((h, first), (h + 1, second)):
            kg.append((kp_ref[at].astype(f32) + mm_nt(v_ref[at], later)).astype(bf16))
            vg.append((vp_ref[at].astype(f32) + mm(k_ref[at], later)).astype(bf16))
    kg_ref[...] = jnp.swapaxes(jnp.stack(kg), 0, 1)
    vg_ref[...] = jnp.swapaxes(jnp.stack(vg), 0, 1)


def final_part(kh, vh, kpart, vpart, later):
    tok = jax.ShapeDtypeStruct((T, HL, E), bf16)
    return pl.pallas_call(
        final_kernel,
        grid=(NC,),
        in_specs=[head_spec()] * 4 + [whole((16, 2, 64, E))],
        out_specs=[tok_spec()] * 2,
        out_shape=[tok] * 2,
        compiler_params=params(),
        cost_estimate=cost(4 * T * HL * E * E, 19 * MIB),
        name="final_part",
    )(kh, vh, kpart, vpart, later)


def swap(pieces):
    return lax.all_to_all(pieces, "seq", 0, 0, tiled=True)


def body(queries, keys, values, out_grad, gain, entry_state):
    mine = lax.axis_index("seq")
    start = lax.dynamic_slice_in_dim(entry_state.reshape(N, 64, E), mine, 1, 0)[0]
    kv = kv_sums(keys, values).reshape(N, 64, E)
    got = swap(kv)
    qh, kh, vh, gh, att, loc = local_part(queries, keys, values, out_grad)
    state = swap(prefix(got, start)).reshape(HL, E, E)
    sums = lax.psum(stats(qh, gh, att, state, gain), "head")
    pre, wloc, w = pre_part(qh, gh, att, state, gain, sums)
    back = swap(w.reshape(N, 64, E))
    normed, query_grad, gv = query_part(qh, kh, vh, pre, att, state, loc, gain, sums)
    rest, total = suffix(back)
    later = swap(rest).reshape(16, 2, 64, E)
    kpart, vpart = keyval_part(qh, kh, vh, pre, gv, wloc)
    key_grad, value_grad = final_part(kh, vh, kpart, vpart, later)
    return normed, query_grad, key_grad, value_grad, total.reshape(HL, 4, E)


def solution(mesh):
    tok = P("seq", "head", None)
    return jax.shard_map(
        body,
        mesh=mesh,
        in_specs=(tok, tok, tok, tok, P("head", None), P("head", None, None)),
        out_specs=(tok, tok, tok, tok, P("head", "seq", None)),
        check_vma=False,
    )
```

```python
import jax
import jax.numpy as jnp
from jax import lax
from jax.experimental import pallas as pl
from jax.experimental.pallas import tpu as pltpu
from jax.sharding import PartitionSpec as P

H = 64
E = 128
T = 768
HL = 16
C = 256
NC = T // C
B = 128
NB = T // B
N = 32
X = 4
WIDTH = H * E
epsilon = 1e-06
f32 = jnp.float32
bf16 = jnp.bfloat16
MIB = 1 << 20


def mm(a, b):
    return lax.dot_general(a, b, (((1,), (0,)), ((), ())), preferred_element_type=f32)


def mm_nt(a, b):
    return lax.dot_general(a, b, (((1,), (1,)), ((), ())), preferred_element_type=f32)


def mm_tn(a, b):
    return lax.dot_general(a, b, (((0,), (0,)), ((), ())), preferred_element_type=f32)


def causal(later=False):
    row = lax.broadcasted_iota(jnp.int32, (C, C), 0)
    col = lax.broadcasted_iota(jnp.int32, (C, C), 1)
    return row <= col if later else col <= row


def heads_first(ref):
    return jnp.swapaxes(ref[...], 0, 1)


def params(vmem=24):
    return pltpu.CompilerParams(vmem_limit_bytes=vmem * MIB)


def cost(flops, moved):
    return pl.CostEstimate(flops=flops, bytes_accessed=moved, transcendentals=0)


HERE = pl.BlockSpec(memory_space=pltpu.VMEM)
ORDER = pl.BlockSpec(memory_space=pl.ANY)
TOK = pl.BlockSpec((C, HL, E), lambda i: (i, 0, 0))
HEAD = pl.BlockSpec((HL, C, E), lambda i: (0, i, 0))
HEAD_BACK = pl.BlockSpec((HL, C, E), lambda i: (0, NC - 1 - i, 0))
CHUNK = pl.BlockSpec((1, HL, E, E), lambda i: (i, 0, 0, 0))
MAJOR = pltpu.HBM((HL, T, E), bf16)
STATES = pltpu.HBM((NC, HL, E, E), bf16)
TOKENS = pltpu.HBM((T, HL, E), bf16)


def rows(step):
    return pl.ds(pl.multiple_of(step * C, C), C)


def far(*arrays):
    return tuple(pltpu.with_memory_space_constraint(a, pltpu.HBM) for a in arrays)


def near(*arrays):
    return tuple(pltpu.with_memory_space_constraint(a, pltpu.VMEM) for a in arrays)


def kv_kernel(k_hbm, v_hbm, o_ref, k_buf, v_buf, sems):
    copies = []
    for i in range(NC):
        at = pl.ds(i * C, C)
        for n, (src, dst) in enumerate(((k_hbm, k_buf), (v_hbm, v_buf))):
            copies.append(pltpu.make_async_copy(src.at[at], dst.at[at], sems.at[i, n]))
            copies[-1].start()
    for i in range(NC):
        copies[2 * i].wait()
        copies[2 * i + 1].wait()
        k = jnp.swapaxes(k_buf[i * C : (i + 1) * C], 0, 1)
        v = jnp.swapaxes(v_buf[i * C : (i + 1) * C], 0, 1)
        for h in range(HL):
            part = mm_tn(k[h], v[h])
            o_ref[h] = part if i == 0 else o_ref[h] + part


def kv_sums(keys, values):
    return pl.pallas_call(
        kv_kernel,
        in_specs=[ORDER, ORDER],
        out_specs=HERE,
        out_shape=pltpu.VMEM((HL, E, E), f32),
        scratch_shapes=[
            pltpu.VMEM((T, HL, E), bf16),
            pltpu.VMEM((T, HL, E), bf16),
            pltpu.SemaphoreType.DMA((NC, 2)),
        ],
        compiler_params=params(32),
        cost_estimate=cost(2 * T * HL * E * E, 7 * MIB),
        name="kv_sums",
    )(*far(keys, values))


def prefix_kernel(r_ref, x_hbm, _, o_ref, x_ref, sem):
    first = pltpu.make_async_copy(x_hbm.at[lax.axis_index("seq")], x_ref, sem)
    first.start()
    first.wait()
    total = x_ref[...]
    for i in range(N):
        o_ref[i] = total
        total = total + r_ref[i]


def prefix(pieces, start, order):
    return pl.pallas_call(
        prefix_kernel,
        in_specs=[HERE, ORDER, ORDER],
        out_specs=HERE,
        out_shape=pltpu.VMEM(pieces.shape, f32),
        scratch_shapes=[pltpu.VMEM((64, E), f32), pltpu.SemaphoreType.DMA],
        compiler_params=params(4),
        cost_estimate=cost(N * 64 * E, 2 * MIB),
        name="prefix",
    )(*near(pieces), *far(start), order)


def suffix_kernel(r_ref, _, o_ref, t_ref):
    total = jnp.zeros_like(t_ref)
    for i in reversed(range(N)):
        o_ref[i] = total
        total = total + r_ref[i]
    t_ref[...] = total


def suffix(pieces, order):
    return pl.pallas_call(
        suffix_kernel,
        in_specs=[HERE, ORDER],
        out_specs=[HERE] * 2,
        out_shape=[
            pltpu.VMEM(pieces.shape, f32),
            jax.ShapeDtypeStruct(pieces.shape[1:], f32),
        ],
        compiler_params=params(4),
        cost_estimate=cost(N * 64 * E, 2 * MIB),
        name="suffix",
    )(*near(pieces), order)


def local_kernel(
    q_ref, k_ref, v_ref, g_ref, _, qh_ref, kh_ref, vh_ref, gh_ref, att_ref, loc_ref, order_ref, acc
):
    @pl.when(pl.program_id(0) == 0)
    def _():
        acc[...] = jnp.zeros_like(acc)
        order_ref[...] = jnp.zeros_like(order_ref)

    mask = causal()
    q = heads_first(q_ref)
    k = heads_first(k_ref)
    v = heads_first(v_ref)
    qh_ref[...] = q
    kh_ref[...] = k
    vh_ref[...] = v
    gh_ref[...] = heads_first(g_ref)
    for h in range(HL):
        qk = jnp.where(mask, mm_nt(q[h], k[h]), 0.0).astype(bf16)
        loc = acc[h].astype(bf16)
        loc_ref[0, h] = loc
        att_ref[h] = (mm(qk, v[h]) + mm(q[h], loc)).astype(bf16)
        acc[h] += mm_tn(k[h], v[h])


def local_part(queries, keys, values, out_grad, order):
    return pl.pallas_call(
        local_kernel,
        grid=(NC,),
        in_specs=[TOK] * 4 + [ORDER],
        out_specs=[HEAD] * 5 + [CHUNK, pl.BlockSpec((8, E), lambda i: (0, 0))],
        out_shape=[MAJOR] * 5 + [STATES, jax.ShapeDtypeStruct((8, E), f32)],
        scratch_shapes=[pltpu.VMEM((HL, E, E), f32)],
        compiler_params=params(32),
        cost_estimate=cost(2 * T * HL * (2 * C * E + 2 * E * E), 30 * MIB),
        name="local_part",
    )(*far(queries, keys, values, out_grad), order)


def stats_kernel(q_ref, g_ref, a_ref, s_ref, gain_ref, att_ref, o_ref, sb_ref):
    step = pl.program_id(0)
    at = rows(step)

    @pl.when(step == 0)
    def _():
        sb_ref[...] = s_ref[...].astype(bf16)

    sq = jnp.zeros((C, E), f32)
    pr = jnp.zeros((C, E), f32)
    for h in range(HL):
        att = a_ref[h, at, :].astype(f32) + mm(q_ref[h, at, :], sb_ref[h])
        att_ref[h, at, :] = att
        up = gain_ref[h : h + 1, :] * g_ref[h, at, :].astype(f32)
        sq = sq + att * att
        pr = pr + up * att
    sq = jnp.sum(sq.T, axis=0, keepdims=True)
    pr = jnp.sum(pr.T, axis=0, keepdims=True)
    for x in range(X):
        o_ref[x, 0:1, :] = sq
        o_ref[x, 1:2, :] = pr


def stats(qh, gh, part, state, gain):
    return pl.pallas_call(
        stats_kernel,
        grid=(NC,),
        in_specs=[HERE] * 5,
        out_specs=[
            HERE,
            pl.BlockSpec((X, 2, C), lambda i: (0, 0, i)),
            pl.BlockSpec((HL, E, E), lambda i: (0, 0, 0)),
        ],
        out_shape=[
            pltpu.VMEM((HL, T, E), f32),
            jax.ShapeDtypeStruct((X, 2, T), f32),
            pltpu.HBM((HL, E, E), bf16),
        ],
        compiler_params=params(12),
        cost_estimate=cost(2 * T * HL * E * E, 10 * MIB),
        name="stats",
    )(*near(qh, gh, part, state, gain))


def scales(sums_ref):
    sums = (sums_ref[0] + sums_ref[1]) + (sums_ref[2] + sums_ref[3])
    rms = jnp.sqrt(sums[0:1, :] / WIDTH + epsilon)
    a = 1.0 / rms
    b = sums[1:2, :] / (WIDTH * rms * rms) * a
    a = jnp.broadcast_to(a, (E, C)).T
    b = jnp.broadcast_to(b, (E, C)).T
    return a, b


def pre_kernel(q_ref, g_ref, a_ref, gain_ref, sums_ref, p_ref, wl_ref, w_ref, acc):
    step = pl.program_id(0)
    at = rows(NC - 1 - step)

    @pl.when(step == 0)
    def _():
        acc[...] = jnp.zeros_like(acc)

    a, b = scales(sums_ref)
    for h in range(HL):
        up = gain_ref[h : h + 1, :] * g_ref[h, at, :].astype(f32)
        p = (up * a - a_ref[h, at, :] * b).astype(bf16)
        p_ref[h] = p
        wl_ref[0, h] = acc[h].astype(bf16)
        acc[h] += mm_tn(q_ref[h, at, :], p)

    @pl.when(step == NC - 1)
    def _():
        low = lax.broadcasted_iota(jnp.int32, (HL, 8, E), 1) < 4
        for h in range(0, HL, 2):
            x = acc[h].reshape(HL, 8, E)
            y = acc[h + 1].reshape(HL, 8, E)
            w_ref[:, 0, 4 * h : 4 * h + 8, :] = jnp.where(low, x, pltpu.roll(y, 4, 1))
            w_ref[:, 1, 4 * h : 4 * h + 8, :] = jnp.where(low, pltpu.roll(x, 4, 1), y)


def pre_part(qh, gh, att, gain, sums):
    return pl.pallas_call(
        pre_kernel,
        grid=(NC,),
        in_specs=[HERE] * 4 + [pl.BlockSpec((X, 2, C), lambda i: (0, 0, NC - 1 - i))],
        out_specs=[
            HEAD_BACK,
            pl.BlockSpec((1, HL, E, E), lambda i: (NC - 1 - i, 0, 0, 0)),
            HERE,
        ],
        out_shape=[MAJOR, STATES, pltpu.VMEM((16, 2, 64, E), f32)],
        scratch_shapes=[pltpu.VMEM((HL, E, E), f32)],
        compiler_params=params(16),
        cost_estimate=cost(4 * T * HL * E * E, 16 * MIB),
        name="pre_part",
    )(*near(qh, gh, att, gain), sums)


def query_kernel(
    q_ref, k_ref, v_ref, p_ref, a_ref, s_ref, loc_ref, gain_ref, sums_ref, n_ref, qg_ref, order_ref
):
    mask = causal()
    order_ref[...] = jnp.zeros_like(order_ref)
    a, _ = scales(sums_ref)
    normed = []
    grads = []
    for h in range(HL):
        state = s_ref[h]
        att = a_ref[h].astype(f32) + mm(q_ref[h], state)
        normed.append((gain_ref[h : h + 1, :] * att * a).astype(bf16))
        p = p_ref[h]
        gv = jnp.where(mask, mm_nt(p, v_ref[h]), 0.0).astype(bf16)
        grads.append((mm_nt(p, state) + mm_nt(p, loc_ref[0, h]) + mm(gv, k_ref[h])).astype(bf16))
    n_ref[...] = jnp.swapaxes(jnp.stack(normed), 0, 1)
    qg_ref[...] = jnp.swapaxes(jnp.stack(grads), 0, 1)


def query_part(qh, kh, vh, pre, part, state, loc, gain, sums):
    return pl.pallas_call(
        query_kernel,
        grid=(NC,),
        in_specs=[HEAD] * 5
        + [
            pl.BlockSpec((HL, E, E), lambda i: (0, 0, 0)),
            CHUNK,
            pl.BlockSpec((HL, E), lambda i: (0, 0)),
            pl.BlockSpec((X, 2, C), lambda i: (0, 0, i)),
        ],
        out_specs=[TOK] * 2 + [pl.BlockSpec((8, E), lambda i: (0, 0))],
        out_shape=[TOKENS] * 2 + [jax.ShapeDtypeStruct((8, E), f32)],
        compiler_params=params(32),
        cost_estimate=cost(2 * T * HL * (2 * C * E + 3 * E * E), 30 * MIB),
        name="query_part",
    )(*far(qh, kh, vh, pre, part, state, loc, gain, sums))


def keyval_kernel(q_ref, k_ref, v_ref, p_ref, wl_ref, _, kg_ref, vg_ref):
    mask = causal(later=True)
    for h in range(HL):
        later = wl_ref[0, h]
        q = q_ref[h]
        k = k_ref[h]
        v = v_ref[h]
        p = p_ref[h]
        kq = jnp.where(mask, mm_nt(k, q), 0.0).astype(bf16)
        vg = jnp.where(mask, mm_nt(v, p), 0.0).astype(bf16)
        kg_ref[h] = (mm(vg, q) + mm_nt(v, later)).astype(bf16)
        vg_ref[h] = (mm(kq, p) + mm(k, later)).astype(bf16)


def keyval_part(qh, kh, vh, pre, wloc, order):
    return pl.pallas_call(
        keyval_kernel,
        grid=(NC,),
        in_specs=[HEAD] * 4 + [CHUNK, ORDER],
        out_specs=[HEAD] * 2,
        out_shape=[MAJOR] * 2,
        compiler_params=params(32),
        cost_estimate=cost(2 * T * HL * (4 * C * E + 2 * E * E), 22 * MIB),
        name="keyval_part",
    )(*far(qh, kh, vh, pre, wloc), order)


def final_kernel(
    k_hbm, v_hbm, kp_hbm, vp_hbm, l_ref, kg_hbm, vg_hbm, k_buf, v_buf, kp_buf, vp_buf, kg_buf, vg_buf, sems, out_sems
):
    copies = []
    for i in range(NB):
        at = pl.ds(i * B, B)
        for n, (src, dst) in enumerate(
            ((k_hbm, k_buf), (v_hbm, v_buf), (kp_hbm, kp_buf), (vp_hbm, vp_buf))
        ):
            copies.append(pltpu.make_async_copy(src.at[:, at], dst.at[:, at], sems.at[i, n]))
            copies[-1].start()
    low = lax.broadcasted_iota(jnp.int32, (HL, 8, E), 1) < 4
    later = []
    for h in range(0, HL, 2):
        even = l_ref[:, 0, 4 * h : 4 * h + 8, :]
        odd = l_ref[:, 1, 4 * h : 4 * h + 8, :]
        later.append(jnp.where(low, even, pltpu.roll(odd, 4, 1)).reshape(E, E).astype(bf16))
        later.append(jnp.where(low, pltpu.roll(even, 4, 1), odd).reshape(E, E).astype(bf16))
    outs = []
    for i in range(NB):
        for n in range(4):
            copies[4 * i + n].wait()
        at = slice(i * B, (i + 1) * B)
        kg = []
        vg = []
        for h in range(HL):
            kg.append((kp_buf[h, at].astype(f32) + mm_nt(v_buf[h, at], later[h])).astype(bf16))
            vg.append((vp_buf[h, at].astype(f32) + mm(k_buf[h, at], later[h])).astype(bf16))
        kg_buf[at] = jnp.swapaxes(jnp.stack(kg), 0, 1)
        vg_buf[at] = jnp.swapaxes(jnp.stack(vg), 0, 1)
        at = pl.ds(i * B, B)
        for n, (src, dst) in enumerate(((kg_buf, kg_hbm), (vg_buf, vg_hbm))):
            outs.append(pltpu.make_async_copy(src.at[at], dst.at[at], out_sems.at[i, n]))
            outs[-1].start()
    for copy in outs:
        copy.wait()


def final_part(kh, vh, kpart, vpart, later):
    return pl.pallas_call(
        final_kernel,
        in_specs=[ORDER] * 4 + [HERE],
        out_specs=[ORDER] * 2,
        out_shape=[TOKENS] * 2,
        scratch_shapes=[pltpu.VMEM((HL, T, E), bf16)] * 4
        + [pltpu.VMEM((T, HL, E), bf16)] * 2
        + [pltpu.SemaphoreType.DMA((NB, 4)), pltpu.SemaphoreType.DMA((NB, 2))],
        compiler_params=params(40),
        cost_estimate=cost(4 * T * HL * E * E, 19 * MIB),
        name="final_part",
    )(*far(kh, vh, kpart, vpart), *near(later))


def swap(pieces):
    return lax.all_to_all(pieces, "seq", 0, 0, tiled=True)


def body(queries, keys, values, out_grad, gain, entry_state):
    start = entry_state.reshape(N, 64, E)
    got = swap(kv_sums(keys, values).reshape(N, 64, E))
    qh, kh, vh, gh, part, loc, order = local_part(queries, keys, values, out_grad, start)
    state = swap(prefix(got, start, order)).reshape(HL, E, E)
    att, sums, state = stats(qh, gh, part, state, gain)
    sums = lax.all_to_all(sums, "head", 0, 0, tiled=True)
    pre, wloc, w = pre_part(qh, gh, att, gain, sums)
    back = swap(w.reshape(N, 64, E))
    normed, query_grad, order = query_part(qh, kh, vh, pre, part, state, loc, gain, sums)
    rest, total = suffix(back, order)
    later = swap(rest).reshape(16, 2, 64, E)
    kpart, vpart = keyval_part(qh, kh, vh, pre, wloc, total)
    key_grad, value_grad = final_part(kh, vh, kpart, vpart, later)
    return normed, query_grad, key_grad, value_grad, total.reshape(HL, 4, E)


def solution(mesh):
    tok = P("seq", "head", None)
    return jax.shard_map(
        body,
        mesh=mesh,
        in_specs=(tok, tok, tok, tok, P("head", None), P("head", None, None)),
        out_specs=(tok, tok, tok, tok, P("head", "seq", None)),
        check_vma=False,
    )
```

```python
import functools

import jax
import jax.numpy as jnp
from jax import lax
from jax.experimental import pallas as pl
from jax.experimental.pallas import tpu as pltpu
from jax.sharding import PartitionSpec as P

H = 64
E = 128
T = 768
HL = 16
C = 256
NC = T // C
B = 128
N = 32
L = 4
HALF = HL // 2
X = 4
WIDTH = H * E
epsilon = 1e-06
f32 = jnp.float32
bf16 = jnp.bfloat16
MIB = 1 << 20


def mm(a, b):
    return lax.dot_general(a, b, (((1,), (0,)), ((), ())), preferred_element_type=f32)


def mm_nt(a, b):
    return lax.dot_general(a, b, (((1,), (1,)), ((), ())), preferred_element_type=f32)


def mm_tn(a, b):
    return lax.dot_general(a, b, (((0,), (0,)), ((), ())), preferred_element_type=f32)


def causal(later=False):
    row = lax.broadcasted_iota(jnp.int32, (C, C), 0)
    col = lax.broadcasted_iota(jnp.int32, (C, C), 1)
    return row <= col if later else col <= row


def heads_first(ref):
    return jnp.swapaxes(ref[...], 0, 1)


def params(vmem=24):
    return pltpu.CompilerParams(vmem_limit_bytes=vmem * MIB)


def cost(flops, moved):
    return pl.CostEstimate(flops=flops, bytes_accessed=moved, transcendentals=0)


HERE = pl.BlockSpec(memory_space=pltpu.VMEM)
ORDER = pl.BlockSpec(memory_space=pl.ANY)
TOK = pl.BlockSpec((C, HL, E), lambda i: (i, 0, 0))
MAJOR = pltpu.VMEM((HL, T, E), bf16)
SQUARES = pltpu.VMEM((HL, T, C), bf16)
STATES = pltpu.VMEM((NC, HL, E, E), bf16)
TOKENS = pltpu.HBM((T, HL, E), bf16)
QUARTER = pltpu.VMEM((HALF * E // L, E), f32)
QUARTERS = pltpu.VMEM((L, HALF * E // L, E), f32)
MARK = pltpu.HBM((8, E), f32)
MARKER = pl.BlockSpec((8, E), lambda i: (0, 0))


def my_place():
    me = lax.axis_index("seq")
    return me // (2 * L), lax.rem(me // 2, L), lax.rem(me, 2)


def far(*arrays):
    return tuple(pltpu.with_memory_space_constraint(a, pltpu.HBM) for a in arrays)


def near(*arrays):
    return tuple(pltpu.with_memory_space_constraint(a, pltpu.VMEM) for a in arrays)


def rows(step):
    return pl.ds(pl.multiple_of(step * C, C), C)


def mm_lower(a, b):
    return jnp.concatenate([mm(a[:B, :B], b[:B]), mm(a[B:], b)], axis=0)


def mm_upper(a, b):
    return jnp.concatenate([mm(a[:B], b), mm(a[B:, B:], b[B:])], axis=0)


def kv_kernel(k_hbm, v_hbm, o_ref, k_buf, v_buf, sems):
    _, _, core = my_place()
    copies = []
    for i in range(NC):
        at = pl.ds(i * C, C)
        for n, (src, dst) in enumerate(((k_hbm, k_buf), (v_hbm, v_buf))):
            copies.append(pltpu.make_async_copy(src.at[at], dst.at[at], sems.at[i, n]))
            copies[-1].start()
    for i in range(NC):
        copies[2 * i].wait()
        copies[2 * i + 1].wait()
        k = jnp.swapaxes(k_buf[i * C : (i + 1) * C], 0, 1)
        v = jnp.swapaxes(v_buf[i * C : (i + 1) * C], 0, 1)
        for h in range(HL):
            part = mm_tn(k[h], v[h])
            half = lax.rem(h // HALF + core, 2)
            o_ref[half, h % HALF] = part if i == 0 else o_ref[half, h % HALF] + part


def kv_sums(keys, values):
    return pl.pallas_call(
        kv_kernel,
        in_specs=[ORDER, ORDER],
        out_specs=HERE,
        out_shape=pltpu.VMEM((2, HALF, E, E), f32),
        scratch_shapes=[
            pltpu.VMEM((T, HL, E), bf16),
            pltpu.VMEM((T, HL, E), bf16),
            pltpu.SemaphoreType.DMA((NC, 2)),
        ],
        compiler_params=params(24),
        cost_estimate=cost(2 * T * HL * E * E, 7 * MIB),
        name="kv_sums",
    )(*far(keys, values))


def pair_kernel(first, m_ref, r_ref, *outs):
    _, z, core = my_place()
    for k in range(L):
        at = lax.rem(z + k, L)
        outs[k][...] = m_ref[at] + r_ref[at]
    outs[L][...] = jnp.where(core == first, m_ref[...], r_ref[...])


def pair(mine, got, first):
    return pl.pallas_call(
        functools.partial(pair_kernel, first),
        in_specs=[HERE] * 2,
        out_specs=[HERE] * (L + 1),
        out_shape=[QUARTER] * L + [QUARTERS],
        compiler_params=params(2),
        cost_estimate=cost(HALF * E * E, 2 * MIB),
        name="pair",
    )(*near(mine, got))


def row_kernel(backward, *refs):
    parts, (_, e_ref, t_ref, buf) = refs[:L], refs[L:]
    _, z, _ = my_place()
    for k in range(L):
        buf[lax.rem(z + L - k, L)] = parts[k][...]
    total = jnp.zeros_like(t_ref)
    for i in reversed(range(L)) if backward else range(L):
        e_ref[i] = total
        total = total + buf[i]
    t_ref[...] = total


def row_sums(parts, order, backward):
    return pl.pallas_call(
        functools.partial(row_kernel, backward),
        in_specs=[HERE] * L + [ORDER],
        out_specs=[HERE] * 2,
        out_shape=[QUARTERS, QUARTER],
        scratch_shapes=[QUARTERS],
        compiler_params=params(2),
        cost_estimate=cost(HALF * E * E, MIB),
        name="row_sums",
    )(*near(*parts), *far(order))


def prior_kernel(e_ref, u1, u2, u3, x_hbm, _, *refs):
    outs, (x_ref, sem) = refs[:L], refs[L:]
    y, z, core = my_place()
    first = pltpu.make_async_copy(x_hbm.at[core * L + z], x_ref, sem)
    first.start()
    first.wait()
    total = x_ref[...]
    for k, u in enumerate((u1, u2, u3)):
        total = total + jnp.where(k + 1 <= y, u[...], 0.0)
    for k in range(L):
        outs[k][...] = total + e_ref[lax.rem(z + k, L)]


def prior_sums(inrow, others, start, order):
    return pl.pallas_call(
        prior_kernel,
        in_specs=[HERE] * L + [ORDER] * 2,
        out_specs=[HERE] * L,
        out_shape=[QUARTER] * L,
        scratch_shapes=[QUARTER, pltpu.SemaphoreType.DMA],
        compiler_params=params(2),
        cost_estimate=cost(HALF * E * E, MIB),
        name="prior_sums",
    )(*near(inrow, *others), *far(start, order))


def later_kernel(e_ref, t_ref, u1, u2, u3, _, *refs):
    outs, (sum_ref, buf) = refs[:L], refs[L:]
    y, z, _ = my_place()
    total = jnp.zeros_like(t_ref)
    for k, u in enumerate((u1, u2, u3)):
        total = total + jnp.where(k + 1 > y, u[...], 0.0)
    for k in range(L):
        outs[k][...] = total + e_ref[lax.rem(z + k, L)]
    buf[...] = (t_ref[...] + u1[...] + u2[...] + u3[...]).reshape(buf.shape)
    sum_ref[...] = buf[y]


def later_sums(inrow, total, others, order):
    return pl.pallas_call(
        later_kernel,
        in_specs=[HERE] * (L + 1) + [ORDER],
        out_specs=[HERE] * (L + 1),
        out_shape=[QUARTER] * L + [jax.ShapeDtypeStruct((HL * L, E), f32)],
        scratch_shapes=[pltpu.VMEM((L, HL * L, E), f32)],
        compiler_params=params(2),
        cost_estimate=cost(HALF * E * E, MIB),
        name="later_sums",
    )(*near(inrow, total, *others), *far(order))


def split_kernel(first, *refs):
    parts, (x_ref, _, own_ref, send_ref) = refs[:L], refs[L:]
    _, z, core = my_place()
    for k in range(L):
        at = lax.rem(z + L - k, L)
        scan = parts[k][...]
        more = scan + x_ref[at]
        own_ref[at] = jnp.where(core == first, scan, more)
        send_ref[at] = jnp.where(core == first, more, scan)


def split(parts, extra, order, first):
    return pl.pallas_call(
        functools.partial(split_kernel, first),
        in_specs=[HERE] * (L + 1) + [ORDER],
        out_specs=[HERE] * 2,
        out_shape=[QUARTERS] * 2,
        compiler_params=params(2),
        cost_estimate=cost(HALF * E * E, 2 * MIB),
        name="split",
    )(*near(*parts, extra), *far(order))


def local_kernel(
    q_ref, k_ref, v_ref, _, qh_ref, kh_ref, vh_ref, att_ref, loc_ref, mark_ref, acc, qk_ref
):
    step = pl.program_id(0)
    at = rows(step)

    @pl.when(step == 0)
    def _():
        acc[...] = jnp.zeros_like(acc)
        mark_ref[...] = jnp.zeros_like(mark_ref)

    mask = causal()
    q = heads_first(q_ref)
    k = heads_first(k_ref)
    v = heads_first(v_ref)
    qh_ref[:, at] = q
    kh_ref[:, at] = k
    vh_ref[:, at] = v
    for h in range(HL):
        qk_ref[h] = jnp.where(mask, mm_nt(q[h], k[h]), 0.0).astype(bf16)
    for h in range(HL):
        loc = acc[h].astype(bf16)
        loc_ref[step, h] = loc
        att_ref[h, at] = (mm_lower(qk_ref[h], v[h]) + mm(q[h], loc)).astype(bf16)
        acc[h] += mm_tn(k[h], v[h])


def local_part(queries, keys, values, order):
    return pl.pallas_call(
        local_kernel,
        grid=(NC,),
        in_specs=[TOK] * 3 + [ORDER],
        out_specs=[HERE] * 5 + [MARKER],
        out_shape=[MAJOR] * 4 + [STATES, MARK],
        scratch_shapes=[pltpu.VMEM((HL, E, E), f32), pltpu.VMEM((HL, C, C), bf16)],
        compiler_params=params(18),
        cost_estimate=cost(2 * T * HL * (2 * C * E + 2 * E * E), 24 * MIB),
        name="local_part",
    )(*far(queries, keys, values, order))


def square_kernel(g_ref, q_ref, k_ref, _, gh_ref, kq_ref, mark_ref):
    at = rows(pl.program_id(0))
    mask = causal(later=True)
    mark_ref[...] = jnp.zeros_like(mark_ref)
    gh_ref[:, at] = heads_first(g_ref)
    for h in range(HL):
        kq_ref[h, at] = jnp.where(mask, mm_nt(k_ref[h, at], q_ref[h, at]), 0.0).astype(bf16)


def square_part(out_grad, qh, kh, order):
    return pl.pallas_call(
        square_kernel,
        grid=(NC,),
        in_specs=[TOK, HERE, HERE, ORDER],
        out_specs=[HERE, HERE, MARKER],
        out_shape=[MAJOR, SQUARES, MARK],
        compiler_params=params(12),
        cost_estimate=cost(2 * T * HL * C * E, 19 * MIB),
        name="square_part",
    )(*far(out_grad), *near(qh, kh), *far(order))


def stats_kernel(q_ref, g_ref, a_ref, own_ref, got_ref, gain_ref, att_ref, o_ref, sb_ref):
    step = pl.program_id(0)
    at = rows(step)

    @pl.when(step == 0)
    def _():
        _, _, core = my_place()
        sb_ref[pl.ds(core * HALF, HALF)] = own_ref[...].astype(bf16)
        sb_ref[pl.ds((1 - core) * HALF, HALF)] = got_ref[...].astype(bf16)

    sq = jnp.zeros((C, E), f32)
    pr = jnp.zeros((C, E), f32)
    for h in range(HL):
        att = a_ref[h, at].astype(f32) + mm(q_ref[h, at], sb_ref[h])
        att_ref[h, at] = att
        up = gain_ref[h : h + 1, :] * g_ref[h, at].astype(f32)
        sq = sq + att * att
        pr = pr + up * att
    sq = jnp.sum(sq.T, axis=0, keepdims=True)
    pr = jnp.sum(pr.T, axis=0, keepdims=True)
    for x in range(X):
        o_ref[x, step, 0:1, :] = sq
        o_ref[x, step, 1:2, :] = pr


def stats(qh, gh, part, own, got, gain):
    return pl.pallas_call(
        stats_kernel,
        grid=(NC,),
        in_specs=[HERE] * 6,
        out_specs=[HERE] * 3,
        out_shape=[
            pltpu.VMEM((HL, T, E), f32),
            pltpu.VMEM((X, NC, 2, C), f32),
            pltpu.VMEM((HL, E, E), bf16),
        ],
        compiler_params=params(8),
        cost_estimate=cost(2 * T * HL * E * E, 10 * MIB),
        name="stats",
    )(*near(qh, gh, part, own, got, gain))


def scales(sums_ref, step):
    sums = (sums_ref[0, step] + sums_ref[1, step]) + (sums_ref[2, step] + sums_ref[3, step])
    rms = jnp.sqrt(sums[0:1, :] / WIDTH + epsilon)
    a = 1.0 / rms
    b = sums[1:2, :] / (WIDTH * rms * rms) * a
    a = jnp.broadcast_to(a, (E, C)).T
    b = jnp.broadcast_to(b, (E, C)).T
    return a, b


def pre_kernel(q_ref, g_ref, a_ref, gain_ref, sums_ref, p_ref, wl_ref, w_ref, other_ref, acc):
    step = pl.program_id(0)
    chunk = NC - 1 - step
    at = rows(chunk)

    @pl.when(step == 0)
    def _():
        acc[...] = jnp.zeros_like(acc)

    a, b = scales(sums_ref, chunk)
    for h in range(HL):
        up = gain_ref[h : h + 1, :] * g_ref[h, at].astype(f32)
        p = (up * a - a_ref[h, at] * b).astype(bf16)
        p_ref[h, at] = p
        wl_ref[chunk, h] = acc[h].astype(bf16)
        acc[h] += mm_tn(q_ref[h, at], p)

    @pl.when(step == NC - 1)
    def _():
        low = lax.broadcasted_iota(jnp.int32, (HL, 8, E), 1) < 4
        _, _, core = my_place()
        for h in range(0, HL, 2):
            x = acc[h].reshape(HL, 8, E)
            y = acc[h + 1].reshape(HL, 8, E)
            even = jnp.where(low, x, pltpu.roll(y, 4, 1))
            odd = jnp.where(low, pltpu.roll(x, 4, 1), y)
            mine = jnp.where(core == 0, even, odd)
            other = jnp.where(core == 0, odd, even)
            for p in range(L * L):
                at = slice(64 * (p // L) + 4 * h, 64 * (p // L) + 4 * h + 8)
                w_ref[p % L, at, :] = mine[p]
                other_ref[p % L, at, :] = other[p]


def pre_part(qh, gh, att, gain, sums):
    return pl.pallas_call(
        pre_kernel,
        grid=(NC,),
        in_specs=[HERE] * 5,
        out_specs=[HERE] * 4,
        out_shape=[MAJOR, STATES, QUARTERS, QUARTERS],
        scratch_shapes=[pltpu.VMEM((HL, E, E), f32)],
        compiler_params=params(8),
        cost_estimate=cost(4 * T * HL * E * E, 16 * MIB),
        name="pre_part",
    )(*near(qh, gh, att, gain, sums))


def query_kernel(
    k_ref, v_ref, p_ref, a_ref, s_ref, loc_ref, gain_ref, sums_ref, _, n_ref, qg_ref, mark_ref, gv_ref
):
    step = pl.program_id(0)
    at = rows(step)
    mask = causal()
    mark_ref[...] = jnp.zeros_like(mark_ref)
    a, _ = scales(sums_ref, step)
    for h in range(HL):
        gv_ref[h] = jnp.where(mask, mm_nt(p_ref[h, at], v_ref[h, at]), 0.0).astype(bf16)
    normed = [(gain_ref[h : h + 1, :] * a_ref[h, at] * a).astype(bf16) for h in range(HL)]
    n_ref[...] = jnp.swapaxes(jnp.stack(normed), 0, 1)
    grads = []
    for h in range(HL):
        p = p_ref[h, at]
        both = mm_nt(
            jnp.concatenate([p, p], axis=1),
            jnp.concatenate([s_ref[h], loc_ref[step, h]], axis=1),
        )
        grads.append((both + mm_lower(gv_ref[h], k_ref[h, at])).astype(bf16))
    qg_ref[...] = jnp.swapaxes(jnp.stack(grads), 0, 1)


def query_part(kh, vh, pre, att, state, loc, gain, sums, order):
    return pl.pallas_call(
        query_kernel,
        grid=(NC,),
        in_specs=[HERE] * 8 + [ORDER],
        out_specs=[TOK] * 2 + [MARKER],
        out_shape=[TOKENS] * 2 + [MARK],
        scratch_shapes=[pltpu.VMEM((HL, C, C), bf16)],
        compiler_params=params(18),
        cost_estimate=cost(2 * T * HL * (2 * C * E + 3 * E * E), 30 * MIB),
        name="query_part",
    )(*near(kh, vh, pre, att, state, loc, gain, sums), *far(order))


def keyval_kernel(q_ref, k_ref, v_ref, p_ref, kq_ref, wl_ref, _, kg_ref, vg_ref, mark_ref, vp_ref):
    step = pl.program_id(0)
    at = rows(step)
    mask = causal(later=True)
    mark_ref[...] = jnp.zeros_like(mark_ref)
    for h in range(HL):
        vp_ref[h] = jnp.where(mask, mm_nt(v_ref[h, at], p_ref[h, at]), 0.0).astype(bf16)
    for h in range(HL):
        later = wl_ref[step, h]
        kg_ref[h, at] = (mm_upper(vp_ref[h], q_ref[h, at]) + mm_nt(v_ref[h, at], later)).astype(bf16)
        vg_ref[h, at] = (mm_upper(kq_ref[h, at], p_ref[h, at]) + mm(k_ref[h, at], later)).astype(bf16)


def keyval_part(qh, kh, vh, pre, kq, wloc, order):
    return pl.pallas_call(
        keyval_kernel,
        grid=(NC,),
        in_specs=[HERE] * 6 + [ORDER],
        out_specs=[HERE] * 2 + [MARKER],
        out_shape=[MAJOR] * 2 + [MARK],
        scratch_shapes=[pltpu.VMEM((HL, C, C), bf16)],
        compiler_params=params(12),
        cost_estimate=cost(2 * T * HL * (3 * C * E + 2 * E * E), 28 * MIB),
        name="keyval_part",
    )(*near(qh, kh, vh, pre, kq, wloc), *far(order))


def final_kernel(k_ref, v_ref, kp_ref, vp_ref, own_ref, got_ref, kg_ref, vg_ref, l_ref):
    step = pl.program_id(0)
    at = rows(step)

    @pl.when(step == 0)
    def _():
        low = lax.broadcasted_iota(jnp.int32, (HL, 8, E), 1) < 4
        _, _, core = my_place()

        def in_order(ref, h):
            parts = []
            for p in range(L * L):
                first = 64 * (p // L) + 4 * h
                parts.append(ref[p % L, first : first + 8, :])
            return jnp.stack(parts)

        for h in range(0, HL, 2):
            own = in_order(own_ref, h)
            got = in_order(got_ref, h)
            even = jnp.where(core == 0, own, got)
            odd = jnp.where(core == 0, got, own)
            l_ref[h] = jnp.where(low, even, pltpu.roll(odd, 4, 1)).reshape(E, E).astype(bf16)
            l_ref[h + 1] = jnp.where(low, pltpu.roll(even, 4, 1), odd).reshape(E, E).astype(bf16)

    kg = []
    for h in range(HL):
        kg.append((kp_ref[h, at].astype(f32) + mm_nt(v_ref[h, at], l_ref[h])).astype(bf16))
    kg_ref[...] = jnp.swapaxes(jnp.stack(kg), 0, 1)
    vg = []
    for h in range(HL):
        vg.append((vp_ref[h, at].astype(f32) + mm(k_ref[h, at], l_ref[h])).astype(bf16))
    vg_ref[...] = jnp.swapaxes(jnp.stack(vg), 0, 1)


def final_part(kh, vh, kpart, vpart, own, got):
    return pl.pallas_call(
        final_kernel,
        grid=(NC,),
        in_specs=[HERE] * 6,
        out_specs=[TOK] * 2,
        out_shape=[TOKENS] * 2,
        scratch_shapes=[pltpu.VMEM((HL, E, E), bf16)],
        compiler_params=params(14),
        cost_estimate=cost(4 * T * HL * E * E, 19 * MIB),
        name="final_part",
    )(*near(kh, vh, kpart, vpart, own, got))


def along(x, move):
    def seq(y, z, core):
        return (y * L + z) * 2 + core

    places = [(y, z, core) for y in range(L) for z in range(L) for core in range(2)]
    return lax.ppermute(x, "seq", [(seq(*p), seq(*move(*p))) for p in places])


def across_cores(x):
    return along(x, lambda y, z, core: (y, z, 1 - core))


def across_z(parts):
    sent = [along(parts[k], lambda y, z, core: (y, (z + k) % L, core)) for k in range(1, L)]
    return [parts[0]] + sent


def across_y(x):
    return [along(x, lambda y, z, core: ((y + k) % L, z, core)) for k in range(1, L)]


def body(queries, keys, values, out_grad, gain, entry_state):
    start = entry_state.reshape(2 * L, HALF * E // L, E)
    kv = kv_sums(keys, values)
    mine, other = (kv[i].reshape(L, HALF * E // L, E) for i in range(2))
    *parts, extra = pair(mine, across_cores(other), 0)
    near_row = across_z(parts)
    qh, kh, vh, part, loc, mark = local_part(queries, keys, values, parts[0])
    inrow, total = row_sums(near_row, mark, False)
    others = across_y(total)
    gh, kq, mark = square_part(out_grad, qh, kh, total)
    scan = across_z(prior_sums(inrow, others, start, mark))
    own, other = split(scan, extra, mark, 0)
    halves = [x.reshape(HALF, E, E) for x in (own, across_cores(other))]
    att, sums, state = stats(qh, gh, part, *halves, gain)
    sums = lax.all_to_all(sums, "head", 0, 0, tiled=True)
    pre, wloc, mine, other = pre_part(qh, gh, att, gain, sums)
    *parts, extra = pair(mine, across_cores(other), 1)
    near_row = across_z(parts)
    normed, query_grad, mark = query_part(kh, vh, pre, att, state, loc, gain, sums, parts[0])
    inrow, total = row_sums(near_row, mark, True)
    others = across_y(total)
    kpart, vpart, mark = keyval_part(qh, kh, vh, pre, kq, wloc, total)
    *parts, entry_grad = later_sums(inrow, total, others, mark)
    own, other = split(across_z(parts), extra, mark, 1)
    key_grad, value_grad = final_part(kh, vh, kpart, vpart, own, across_cores(other))
    return normed, query_grad, key_grad, value_grad, entry_grad.reshape(HL, L, E)


def solution(mesh):
    tok = P("seq", "head", None)
    return jax.shard_map(
        body,
        mesh=mesh,
        in_specs=(tok, tok, tok, tok, P("head", None), P("head", None, None)),
        out_specs=(tok, tok, tok, tok, P("head", "seq", None)),
        check_vma=False,
    )
```

```python
import functools

import jax
import jax.numpy as jnp
from jax import lax
from jax.experimental import pallas as pl
from jax.experimental.pallas import tpu as pltpu
from jax.sharding import PartitionSpec as P

H = 64
E = 128
T = 768
HL = 16
C = 256
NC = T // C
B = 128
NB = T // B
AHEAD = 3
ZSTEPS = (0, 2, 1, 3)
YSTEPS = (1, 3, 2)
N = 32
L = 4
HALF = HL // 2
X = 4
WIDTH = H * E
epsilon = 1e-06
f32 = jnp.float32
bf16 = jnp.bfloat16
MIB = 1 << 20


def mm(a, b):
    return lax.dot_general(a, b, (((1,), (0,)), ((), ())), preferred_element_type=f32)


def mm_nt(a, b):
    return lax.dot_general(a, b, (((1,), (1,)), ((), ())), preferred_element_type=f32)


def mm_tn(a, b):
    return lax.dot_general(a, b, (((0,), (0,)), ((), ())), preferred_element_type=f32)


def causal(later=False):
    row = lax.broadcasted_iota(jnp.int32, (C, C), 0)
    col = lax.broadcasted_iota(jnp.int32, (C, C), 1)
    return row <= col if later else col <= row


def heads_first(ref):
    return jnp.swapaxes(ref[...], 0, 1)


def params(vmem=24):
    return pltpu.CompilerParams(vmem_limit_bytes=vmem * MIB)


def cost(flops, moved):
    return pl.CostEstimate(flops=flops, bytes_accessed=moved, transcendentals=0)


HERE = pl.BlockSpec(memory_space=pltpu.VMEM)
AWAY = pl.BlockSpec(memory_space=pl.ANY)
TOK = pl.BlockSpec((C, HL, E), lambda i: (i, 0, 0))
MAJOR = pltpu.VMEM((HL, T, E), bf16)
SQUARES = pltpu.VMEM((HL, T, C), bf16)
STATES = pltpu.VMEM((NC, HL, E, E), bf16)
TOKENS = pltpu.HBM((T, HL, E), bf16)
QUARTER = pltpu.VMEM((HALF * E // L, E), f32)
QUARTERS = pltpu.VMEM((L, HALF * E // L, E), f32)
MARK = pltpu.VMEM((8, E), f32)


def my_place():
    me = lax.axis_index("seq")
    return me // (2 * L), lax.rem(me // 2, L), lax.rem(me, 2)


def my_heads():
    _, _, core = my_place()
    return core * HALF, (1 - core) * HALF


def far(*arrays):
    return tuple(pltpu.with_memory_space_constraint(a, pltpu.HBM) for a in arrays)


def near(*arrays):
    return tuple(pltpu.with_memory_space_constraint(a, pltpu.VMEM) for a in arrays)


def rows(step):
    return pl.ds(pl.multiple_of(step * C, C), C)


def mm_lower(a, b):
    return jnp.concatenate([mm(a[:B, :B], b[:B]), mm(a[B:], b)], axis=0)


def mm_upper(a, b):
    return jnp.concatenate([mm(a[:B], b), mm(a[B:, B:], b[B:])], axis=0)


def kv_other_kernel(k_hbm, v_hbm, kh_ref, vh_ref, o_ref, k_buf, v_buf, sems):
    _, other = my_heads()
    copies = []
    for i in range(NB):
        at = pl.ds(i * B, B)
        for n, (src, dst) in enumerate(((k_hbm, k_buf), (v_hbm, v_buf))):
            copies.append(pltpu.make_async_copy(src.at[at], dst.at[at], sems.at[i, n]))
    for copy in copies[: 2 * AHEAD]:
        copy.start()
    for i in range(NB):
        at = slice(i * B, (i + 1) * B)
        copies[2 * i].wait()
        copies[2 * i + 1].wait()
        for copy in copies[2 * (i + AHEAD) : 2 * (i + AHEAD) + 2]:
            copy.start()
        kh_ref[:, at] = jnp.swapaxes(k_buf[at], 0, 1)
        vh_ref[:, at] = jnp.swapaxes(v_buf[at], 0, 1)
        for j in range(HALF):
            part = mm_tn(kh_ref[other + j, at], vh_ref[other + j, at])
            o_ref[j] = part if i == 0 else o_ref[j] + part


def kv_other(keys, values):
    return pl.pallas_call(
        kv_other_kernel,
        in_specs=[AWAY, AWAY],
        out_specs=[HERE] * 3,
        out_shape=[MAJOR] * 2 + [pltpu.VMEM((HALF, E, E), f32)],
        scratch_shapes=[
            pltpu.VMEM((T, HL, E), bf16),
            pltpu.VMEM((T, HL, E), bf16),
            pltpu.SemaphoreType.DMA((NB, 2)),
        ],
        compiler_params=params(24),
        cost_estimate=cost(T * HL * E * E, 7 * MIB),
        name="kv_other",
    )(*far(keys, values))


def kv_mine_kernel(k_ref, v_ref, o_ref):
    mine, _ = my_heads()
    for j in range(HALF):
        o_ref[j] = mm_tn(k_ref[mine + j], v_ref[mine + j])


def kv_mine(kh, vh):
    return pl.pallas_call(
        kv_mine_kernel,
        in_specs=[HERE] * 2,
        out_specs=HERE,
        out_shape=pltpu.VMEM((HALF, E, E), f32),
        compiler_params=params(4),
        cost_estimate=cost(T * HL * E * E, MIB),
        name="kv_mine",
    )(*near(kh, vh))


def pair_kernel(first, m_ref, r_ref, *outs):
    _, z, core = my_place()
    for out, k in zip(outs, ZSTEPS):
        at = lax.rem(z + k, L)
        out[...] = m_ref[at] + r_ref[at]
    outs[L][...] = jnp.where(core == first, m_ref[...], r_ref[...])


def pair(mine, got, first):
    return pl.pallas_call(
        functools.partial(pair_kernel, first),
        in_specs=[HERE] * 2,
        out_specs=[HERE] * (L + 1),
        out_shape=[QUARTER] * L + [QUARTERS],
        compiler_params=params(2),
        cost_estimate=cost(HALF * E * E, 2 * MIB),
        name="pair",
    )(*near(mine, got))


def row_kernel(backward, *refs):
    parts, (_, e_ref, t_ref, buf) = refs[:L], refs[L:]
    _, z, _ = my_place()
    for part, k in zip(parts, ZSTEPS):
        buf[lax.rem(z + L - k, L)] = part[...]
    total = jnp.zeros_like(t_ref)
    for i in reversed(range(L)) if backward else range(L):
        e_ref[i] = total
        total = total + buf[i]
    t_ref[...] = total


def row_sums(parts, order, backward):
    return pl.pallas_call(
        functools.partial(row_kernel, backward),
        in_specs=[HERE] * (L + 1),
        out_specs=[HERE] * 2,
        out_shape=[QUARTERS, QUARTER],
        scratch_shapes=[QUARTERS],
        compiler_params=params(2),
        cost_estimate=cost(HALF * E * E, MIB),
        name="row_sums",
    )(*near(*parts, order))


def prior_kernel(e_ref, u1, u2, u3, x_ref, _, *outs):
    y, z, _ = my_place()
    total = x_ref[...]
    for k, u in zip(YSTEPS, (u1, u2, u3)):
        total = total + jnp.where(k <= y, u[...], 0.0)
    for out, k in zip(outs, ZSTEPS):
        out[...] = total + e_ref[lax.rem(z + k, L)]


def prior_sums(inrow, others, start, order):
    return pl.pallas_call(
        prior_kernel,
        in_specs=[HERE] * (L + 2),
        out_specs=[HERE] * L,
        out_shape=[QUARTER] * L,
        compiler_params=params(2),
        cost_estimate=cost(HALF * E * E, MIB),
        name="prior_sums",
    )(*near(inrow, *others, start, order))


def later_kernel(e_ref, t_ref, u1, u2, u3, _, *refs):
    outs, (keep_ref, send_ref, buf) = refs[:L], refs[L:]
    y, z, core = my_place()
    total = jnp.zeros_like(t_ref)
    for k, u in zip(YSTEPS, (u1, u2, u3)):
        total = total + jnp.where(k > y, u[...], 0.0)
    for out, k in zip(outs, ZSTEPS):
        out[...] = total + e_ref[lax.rem(z + k, L)]
    buf[...] = (t_ref[...] + u1[...] + u2[...] + u3[...]).reshape(buf.shape)
    low = lax.broadcasted_iota(jnp.int32, (8, E), 0) < 4
    for j in range(0, HALF, 2):
        a = buf[y, 8 * j : 8 * j + 8]
        b = buf[y, 8 * j + 8 : 8 * j + 16]
        even = jnp.where(low, a, pltpu.roll(b, 4, 0))
        odd = jnp.where(low, pltpu.roll(a, 4, 0), b)
        keep_ref[4 * j : 4 * j + 8] = jnp.where(core == 0, even, odd)
        send_ref[4 * j : 4 * j + 8] = jnp.where(core == 0, odd, even)


def later_sums(inrow, total, others, order):
    return pl.pallas_call(
        later_kernel,
        in_specs=[HERE] * (L + 2),
        out_specs=[HERE] * (L + 2),
        out_shape=[QUARTER] * L + [pltpu.VMEM((HALF * L, E), f32)] * 2,
        scratch_shapes=[pltpu.VMEM((L, HALF * 8, E), f32)],
        compiler_params=params(2),
        cost_estimate=cost(HALF * E * E, MIB),
        name="later_sums",
    )(*near(inrow, total, *others, order))


def split_kernel(first, *refs):
    parts, (x_ref, _, own_ref, send_ref) = refs[:L], refs[L:]
    _, z, core = my_place()
    for part, k in zip(parts, ZSTEPS):
        at = lax.rem(z + L - k, L)
        scan = part[...]
        more = scan + x_ref[at]
        own_ref[at] = jnp.where(core == first, scan, more)
        send_ref[at] = jnp.where(core == first, more, scan)


def split(parts, extra, order, first):
    return pl.pallas_call(
        functools.partial(split_kernel, first),
        in_specs=[HERE] * (L + 2),
        out_specs=[HERE] * 2,
        out_shape=[QUARTERS] * 2,
        compiler_params=params(2),
        cost_estimate=cost(HALF * E * E, 2 * MIB),
        name="split",
    )(*near(*parts, extra, order))


def local_kernel(
    q_ref, g_ref, k_ref, v_ref, x_hbm, _, qh_ref, gh_ref, loc_ref, x_ref, mark_ref, acc, sem
):
    step = pl.program_id(0)
    at = rows(step)
    _, z, core = my_place()
    quarter = pltpu.make_async_copy(x_hbm.at[core * L + z], x_ref, sem)

    @pl.when(step == 0)
    def _():
        quarter.start()
        acc[...] = jnp.zeros_like(acc)
        mark_ref[...] = jnp.zeros_like(mark_ref)

    qh_ref[:, at] = heads_first(q_ref)
    gh_ref[:, at] = heads_first(g_ref)
    loc_ref[step] = acc[...].astype(bf16)

    @pl.when(step < NC - 1)
    def _():
        for h in range(HL):
            acc[h] += mm_tn(k_ref[h, at], v_ref[h, at])

    @pl.when(step == NC - 1)
    def _():
        quarter.wait()


def local_states(queries, out_grad, kh, vh, start, order):
    return pl.pallas_call(
        local_kernel,
        grid=(NC,),
        in_specs=[TOK] * 2 + [HERE] * 2 + [AWAY, HERE],
        out_specs=[HERE] * 5,
        out_shape=[MAJOR] * 2 + [STATES, QUARTER, MARK],
        scratch_shapes=[pltpu.VMEM((HL, E, E), f32), pltpu.SemaphoreType.DMA],
        compiler_params=params(12),
        cost_estimate=cost(2 * T * HL * E * E, 12 * MIB),
        name="local_states",
    )(*far(queries, out_grad), *near(kh, vh), *far(start), *near(order))


def inner_kernel(q_ref, k_ref, v_ref, loc_ref, _, att_ref, mark_ref, qk_ref):
    step = pl.program_id(0)
    at = rows(step)
    mask = causal()
    mark_ref[...] = jnp.zeros_like(mark_ref)
    for h in range(HL):
        qk_ref[h] = jnp.where(mask, mm_nt(q_ref[h, at], k_ref[h, at]), 0.0).astype(bf16)
    for h in range(HL):
        att = mm_lower(qk_ref[h], v_ref[h, at]) + mm(q_ref[h, at], loc_ref[step, h])
        att_ref[h, at] = att.astype(bf16)


def inner_part(qh, kh, vh, loc, order):
    return pl.pallas_call(
        inner_kernel,
        grid=(NC,),
        in_specs=[HERE] * 5,
        out_specs=[HERE] * 2,
        out_shape=[MAJOR, MARK],
        scratch_shapes=[pltpu.VMEM((HL, C, C), bf16)],
        compiler_params=params(8),
        cost_estimate=cost(2 * T * HL * (2 * C * E + E * E), 16 * MIB),
        name="inner_part",
    )(*near(qh, kh, vh, loc, order))


def square_kernel(q_ref, k_ref, _, kq_ref, mark_ref):
    at = rows(pl.program_id(0))
    mask = causal(later=True)
    mark_ref[...] = jnp.zeros_like(mark_ref)
    for h in range(HL):
        kq_ref[h, at] = jnp.where(mask, mm_nt(k_ref[h, at], q_ref[h, at]), 0.0).astype(bf16)


def square_part(qh, kh, order):
    return pl.pallas_call(
        square_kernel,
        grid=(NC,),
        in_specs=[HERE] * 3,
        out_specs=[HERE] * 2,
        out_shape=[SQUARES, MARK],
        compiler_params=params(4),
        cost_estimate=cost(2 * T * HL * C * E, 12 * MIB),
        name="square_part",
    )(*near(qh, kh, order))


def stats_half(first, h, state, refs, sq, pr, at):
    q_ref, g_ref, a_ref, gain_ref, att_ref = refs
    for j in range(HALF):
        att = a_ref[h + j, at].astype(f32) + mm(q_ref[h + j, at], state[j])
        att_ref[h + j, at] = att
        up = gain_ref[pl.ds(h + j, 1), :] * g_ref[h + j, at].astype(f32)
        sq = sq + att * att
        pr = pr + up * att
    return sq, pr


def stats_own_kernel(q_ref, g_ref, a_ref, own_ref, gain_ref, att_ref, sb_ref, sum_ref):
    step = pl.program_id(0)
    at = rows(step)
    mine, _ = my_heads()

    @pl.when(step == 0)
    def _():
        sb_ref[pl.ds(mine, HALF)] = own_ref[...].astype(bf16)

    state = [sb_ref[mine + j] for j in range(HALF)]
    zero = jnp.zeros((C, E), f32)
    refs = (q_ref, g_ref, a_ref, gain_ref, att_ref)
    sum_ref[0, at], sum_ref[1, at] = stats_half(0, mine, state, refs, zero, zero, at)


def stats_got_kernel(
    q_ref, g_ref, a_ref, got_ref, gain_ref, sum_ref, _, __, att_ref, sb_ref, o_ref
):
    step = pl.program_id(0)
    at = rows(step)
    _, other = my_heads()

    @pl.when(step == 0)
    def _():
        sb_ref[pl.ds(other, HALF)] = got_ref[...].astype(bf16)

    state = [sb_ref[other + j] for j in range(HALF)]
    refs = (q_ref, g_ref, a_ref, gain_ref, att_ref)
    sq, pr = stats_half(1, other, state, refs, sum_ref[0, at], sum_ref[1, at], at)
    o_ref[step, 0:1, :] = jnp.sum(sq.T, axis=0, keepdims=True)
    o_ref[step, 1:2, :] = jnp.sum(pr.T, axis=0, keepdims=True)


ATTENDED = pltpu.VMEM((HL, T, E), f32)
STATE = pltpu.VMEM((HL, E, E), bf16)


def stats_own(qh, gh, part, own, gain):
    return pl.pallas_call(
        stats_own_kernel,
        grid=(NC,),
        in_specs=[HERE] * 5,
        out_specs=[HERE] * 3,
        out_shape=[ATTENDED, STATE, pltpu.VMEM((2, T, E), f32)],
        compiler_params=params(6),
        cost_estimate=cost(T * HL * E * E, 5 * MIB),
        name="stats_own",
    )(*near(qh, gh, part, own, gain))


def stats_got(qh, gh, part, got, gain, sums, att, state):
    return pl.pallas_call(
        stats_got_kernel,
        grid=(NC,),
        in_specs=[HERE] * 8,
        out_specs=[HERE] * 3,
        out_shape=[ATTENDED, STATE, pltpu.VMEM((NC, 2, C), f32)],
        input_output_aliases={6: 0, 7: 1},
        compiler_params=params(6),
        cost_estimate=cost(T * HL * E * E, 5 * MIB),
        name="stats_got",
    )(*near(qh, gh, part, got, gain, sums, att, state))


def scales(sums, step):
    sums = (sums[0][step] + sums[1][step]) + (sums[2][step] + sums[3][step])
    rms = jnp.sqrt(sums[0:1, :] / WIDTH + epsilon)
    a = 1.0 / rms
    b = sums[1:2, :] / (WIDTH * rms * rms) * a
    a = jnp.broadcast_to(a, (E, C)).T
    b = jnp.broadcast_to(b, (E, C)).T
    return a, b


def pre_kernel(own, q_ref, g_ref, a_ref, gain_ref, s0, s1, s2, s3, *refs):
    p_ref, wl_ref, w_ref, acc = refs[-4:]
    step = pl.program_id(0)
    chunk = NC - 1 - step
    at = rows(chunk)
    first = my_heads()[0 if own else 1]

    @pl.when(step == 0)
    def _():
        acc[...] = jnp.zeros_like(acc)

    a, b = scales((s0, s1, s2, s3), chunk)
    wl_ref[chunk, pl.ds(first, HALF)] = acc[...].astype(bf16)
    for j in range(HALF):
        h = first + j
        up = gain_ref[pl.ds(h, 1), :] * g_ref[h, at].astype(f32)
        p = (up * a - a_ref[h, at] * b).astype(bf16)
        p_ref[h, at] = p
        acc[j] += mm_tn(q_ref[h, at], p)

    @pl.when(step == NC - 1)
    def _():
        for j in range(HALF):
            x = acc[j]
            for n in range(L * L):
                to = slice(64 * (n // L) + 8 * j, 64 * (n // L) + 8 * j + 8)
                w_ref[n % L, to, :] = x[8 * n : 8 * n + 8]


def pre_part(qh, gh, att, gain, sums, *half_done):
    own = len(half_done) > 0
    return pl.pallas_call(
        functools.partial(pre_kernel, own),
        grid=(NC,),
        in_specs=[HERE] * (8 + len(half_done)),
        out_specs=[HERE] * 3,
        out_shape=[MAJOR, STATES, QUARTERS],
        input_output_aliases={8: 0, 9: 1} if own else {},
        scratch_shapes=[pltpu.VMEM((HALF, E, E), f32)],
        compiler_params=params(6),
        cost_estimate=cost(T * HL * E * E, 8 * MIB),
        name="pre_own" if own else "pre_other",
    )(*near(qh, gh, att, gain, *sums, *half_done))


def query_kernel(k_ref, v_ref, p_ref, s_ref, loc_ref, _, qg_ref, mark_ref, gv_ref, sum_ref):
    step = pl.program_id(0)
    at = rows(step)
    mask = causal()
    mark_ref[...] = jnp.zeros_like(mark_ref)
    for h in range(HL):
        gv_ref[h] = jnp.where(mask, mm_nt(p_ref[h, at], v_ref[h, at]), 0.0).astype(bf16)
    for h in range(HL):
        p = p_ref[h, at]
        sum_ref[h] = mm_nt(
            jnp.concatenate([p, p], axis=1),
            jnp.concatenate([s_ref[h], loc_ref[step, h]], axis=1),
        )
    for h in range(HL):
        qg_ref[h, at] = (sum_ref[h] + mm_lower(gv_ref[h], k_ref[h, at])).astype(bf16)


def query_part(kh, vh, pre, state, loc, order):
    return pl.pallas_call(
        query_kernel,
        grid=(NC,),
        in_specs=[HERE] * 6,
        out_specs=[HERE] * 2,
        out_shape=[MAJOR, MARK],
        scratch_shapes=[pltpu.VMEM((HL, C, C), bf16), pltpu.VMEM((HL, C, E), f32)],
        compiler_params=params(8),
        cost_estimate=cost(2 * T * HL * (2 * C * E + 2 * E * E), 16 * MIB),
        name="query_part",
    )(*near(kh, vh, pre, state, loc, order))


def key_kernel(q_ref, v_ref, p_ref, wl_ref, _, kg_ref, mark_ref, vp_ref, sum_ref):
    step = pl.program_id(0)
    at = rows(step)
    mask = causal(later=True)
    mark_ref[...] = jnp.zeros_like(mark_ref)
    for h in range(HL):
        vp_ref[h] = jnp.where(mask, mm_nt(v_ref[h, at], p_ref[h, at]), 0.0).astype(bf16)
    for h in range(HL):
        sum_ref[h] = mm_nt(v_ref[h, at], wl_ref[step, h])
    for h in range(HL):
        kg_ref[h, at] = (sum_ref[h] + mm_upper(vp_ref[h], q_ref[h, at])).astype(bf16)


def key_part(qh, vh, pre, wloc, order):
    return pl.pallas_call(
        key_kernel,
        grid=(NC,),
        in_specs=[HERE] * 5,
        out_specs=[HERE] * 2,
        out_shape=[MAJOR, MARK],
        scratch_shapes=[pltpu.VMEM((HL, C, C), bf16), pltpu.VMEM((HL, C, E), f32)],
        compiler_params=params(8),
        cost_estimate=cost(2 * T * HL * (2 * C * E + E * E), 16 * MIB),
        name="key_part",
    )(*near(qh, vh, pre, wloc, order))


def value_kernel(
    k_ref, p_ref, kq_ref, wl_ref, a_ref, qh_ref, gain_ref, s0, s1, s2, s3, _, n_ref, qg_ref, vg_ref, mark_ref
):
    step = pl.program_id(0)
    at = rows(step)
    mark_ref[...] = jnp.zeros_like(mark_ref)
    a, _ = scales((s0, s1, s2, s3), step)
    normed = [(gain_ref[h : h + 1, :] * a_ref[h, at] * a).astype(bf16) for h in range(HL)]
    n_ref[...] = jnp.swapaxes(jnp.stack(normed), 0, 1)
    qg_ref[...] = jnp.swapaxes(qh_ref[:, at], 0, 1)
    for h in range(HL):
        part = mm_upper(kq_ref[h, at], p_ref[h, at]) + mm(k_ref[h, at], wl_ref[step, h])
        vg_ref[h, at] = part.astype(bf16)


def value_part(kh, pre, kq, wloc, att, grad, gain, sums, order):
    return pl.pallas_call(
        value_kernel,
        grid=(NC,),
        in_specs=[HERE] * 12,
        out_specs=[TOK, TOK, HERE, HERE],
        out_shape=[TOKENS, TOKENS, MAJOR, MARK],
        compiler_params=params(14),
        cost_estimate=cost(2 * T * HL * (C * E + E * E), 20 * MIB),
        name="value_part",
    )(*near(kh, pre, kq, wloc, att, grad, gain, *sums, order))


def final_half(first, l_ref, k_ref, v_ref, kg_ref, vg_ref, at):
    for j in range(HALF):
        h = first + j
        kg_ref[h, at] = (kg_ref[h, at].astype(f32) + mm_nt(v_ref[h, at], l_ref[j])).astype(bf16)
    for j in range(HALF):
        h = first + j
        vg_ref[h, at] = (vg_ref[h, at].astype(f32) + mm(k_ref[h, at], l_ref[j])).astype(bf16)


def in_order(l_ref, x_ref):
    for j in range(HALF):
        parts = []
        for n in range(L * L):
            first = 64 * (n // L) + 8 * j
            parts.append(x_ref[n % L, first : first + 8, :])
        l_ref[j] = jnp.concatenate(parts, axis=0).astype(bf16)


def final_own_kernel(k_ref, v_ref, own_ref, _, __, kg_ref, vg_ref, l_ref):
    step = pl.program_id(0)

    @pl.when(step == 0)
    def _():
        in_order(l_ref, own_ref)

    final_half(my_heads()[0], l_ref, k_ref, v_ref, kg_ref, vg_ref, rows(step))


def final_own(kh, vh, own, kpart, vpart):
    return pl.pallas_call(
        final_own_kernel,
        grid=(NC,),
        in_specs=[HERE] * 5,
        out_specs=[HERE] * 2,
        out_shape=[MAJOR] * 2,
        input_output_aliases={3: 0, 4: 1},
        scratch_shapes=[pltpu.VMEM((HALF, E, E), bf16)],
        compiler_params=params(4),
        cost_estimate=cost(2 * T * HL * E * E, 8 * MIB),
        name="final_own",
    )(*near(kh, vh, own, kpart, vpart))


def final_got_kernel(
    k_ref, v_ref, got_ref, kp_ref, vp_ref, mine_ref, theirs_ref, kg_ref, vg_ref, e_ref, l_ref
):
    step = pl.program_id(0)
    at = rows(step)
    mine, other = my_heads()

    @pl.when(step == 0)
    def _():
        in_order(l_ref, got_ref)
        e_ref[pl.ds(pl.multiple_of(mine * L, 8), HALF * L)] = mine_ref[...]
        e_ref[pl.ds(pl.multiple_of(other * L, 8), HALF * L)] = theirs_ref[...]

    final_half(other, l_ref, k_ref, v_ref, kp_ref, vp_ref, at)
    kg_ref[...] = jnp.swapaxes(kp_ref[:, at], 0, 1)
    vg_ref[...] = jnp.swapaxes(vp_ref[:, at], 0, 1)


def final_got(kh, vh, got, kpart, vpart, mine, theirs):
    return pl.pallas_call(
        final_got_kernel,
        grid=(NC,),
        in_specs=[HERE] * 7,
        out_specs=[TOK] * 2 + [HERE],
        out_shape=[TOKENS] * 2 + [jax.ShapeDtypeStruct((HL * L, E), f32)],
        scratch_shapes=[pltpu.VMEM((HALF, E, E), bf16)],
        compiler_params=params(14),
        cost_estimate=cost(2 * T * HL * E * E, 15 * MIB),
        name="final_got",
    )(*near(kh, vh, got, kpart, vpart, mine, theirs))


def along(x, move):
    def seq(y, z, core):
        return (y * L + z) * 2 + core

    places = [(y, z, core) for y in range(L) for z in range(L) for core in range(2)]
    return lax.ppermute(x, "seq", [(seq(*p), seq(*move(*p))) for p in places])


def across_cores(x):
    return along(x, lambda y, z, core: (y, z, 1 - core))


def across_z(parts):
    return list(parts[:1]) + [
        along(x, lambda y, z, core: (y, (z + k) % L, core)) for x, k in zip(parts[1:], ZSTEPS[1:])
    ]


def across_y(x):
    return [along(x, lambda y, z, core: ((y + k) % L, z, core)) for k in YSTEPS]


def across_heads(x):
    return [x] + [lax.ppermute(x, "head", [(i, (i + k) % X) for i in range(X)]) for k in range(1, X)]


def body(queries, keys, values, out_grad, gain, entry_state):
    rows_of = HALF * E // L
    start = entry_state.reshape(2 * L, rows_of, E)
    kh, vh, other = kv_other(keys, values)
    got = across_cores(other.reshape(L, rows_of, E))
    *parts, extra = pair(kv_mine(kh, vh).reshape(L, rows_of, E), got, 0)
    near_row = across_z(parts)
    qh, gh, loc, start, mark = local_states(queries, out_grad, kh, vh, start, parts[0])
    inrow, total = row_sums(near_row, mark, False)
    others = across_y(total)
    part, mark = inner_part(qh, kh, vh, loc, total)
    parts = prior_sums(inrow, others, start, mark)
    scan = across_z(parts)
    kq, mark = square_part(qh, kh, parts[0])
    own, other = split(scan, extra, mark, 0)
    got = across_cores(other)
    att, state, sums = stats_own(qh, gh, part, own.reshape(HALF, E, E), gain)
    got = got.reshape(HALF, E, E)
    att, state, sums = stats_got(qh, gh, part, got, gain, sums, att, state)
    sums = across_heads(sums)
    pre, wloc, other = pre_part(qh, gh, att, gain, sums)
    got = across_cores(other)
    pre, wloc, mine = pre_part(qh, gh, att, gain, sums, pre, wloc)
    *parts, extra = pair(mine, got, 1)
    near_row = across_z(parts)
    grad, mark = query_part(kh, vh, pre, state, loc, parts[0])
    inrow, total = row_sums(near_row, mark, True)
    others = across_y(total)
    kpart, mark = key_part(qh, vh, pre, wloc, total)
    *parts, mine, theirs = later_sums(inrow, total, others, mark)
    scan = across_z(parts)
    theirs = across_cores(theirs)
    normed, query_grad, vpart, mark = value_part(
        kh, pre, kq, wloc, att, grad, gain, sums, parts[0]
    )
    own, other = split(scan, extra, mark, 1)
    got = across_cores(other)
    kpart, vpart = final_own(kh, vh, own, kpart, vpart)
    key_grad, value_grad, entry_grad = final_got(kh, vh, got, kpart, vpart, mine, theirs)
    return normed, query_grad, key_grad, value_grad, entry_grad.reshape(HL, L, E)


def solution(mesh):
    tok = P("seq", "head", None)
    return jax.shard_map(
        body,
        mesh=mesh,
        in_specs=(tok, tok, tok, tok, P("head", None), P("head", None, None)),
        out_specs=(tok, tok, tok, tok, P("head", "seq", None)),
        check_vma=False,
    )
```

```python
import functools

import jax
import jax.numpy as jnp
from jax import lax
from jax.experimental import pallas as pl
from jax.experimental.pallas import tpu as pltpu
from jax.sharding import PartitionSpec as P

H = 64
E = 128
T = 768
HL = 16
C = 256
NC = T // C
B = 128
NB = T // B
ZSTEPS = (0, 2, 3, 1)
YSTEPS = (3, 1, 2)
N = 32
L = 4
HALF = HL // 2
X = 4
WIDTH = H * E
epsilon = 1e-06
f32 = jnp.float32
bf16 = jnp.bfloat16
MIB = 1 << 20


def mm(a, b):
    return lax.dot_general(a, b, (((1,), (0,)), ((), ())), preferred_element_type=f32)


def mm_nt(a, b):
    return lax.dot_general(a, b, (((1,), (1,)), ((), ())), preferred_element_type=f32)


def mm_tn(a, b):
    return lax.dot_general(a, b, (((0,), (0,)), ((), ())), preferred_element_type=f32)


def causal(later=False):
    row = lax.broadcasted_iota(jnp.int32, (C, C), 0)
    col = lax.broadcasted_iota(jnp.int32, (C, C), 1)
    return row <= col if later else col <= row


def heads_first(ref):
    return jnp.swapaxes(ref[...], 0, 1)


def params(vmem=24):
    return pltpu.CompilerParams(vmem_limit_bytes=vmem * MIB)


def cost(flops, moved):
    return pl.CostEstimate(flops=flops, bytes_accessed=moved, transcendentals=0)


HERE = pl.BlockSpec(memory_space=pltpu.VMEM)
AWAY = pl.BlockSpec(memory_space=pl.ANY)
TOK = pl.BlockSpec((C, HL, E), lambda i: (i, 0, 0))
MAJOR = pltpu.VMEM((HL, T, E), bf16)
SQUARES = pltpu.VMEM((HL, T, C), bf16)
STATES = pltpu.VMEM((NC, HL, E, E), bf16)
TOKENS = pltpu.HBM((T, HL, E), bf16)
QUARTER = pltpu.VMEM((HALF * E // L, E), f32)
QUARTERS = pltpu.VMEM((L, HALF * E // L, E), f32)
MARK = pltpu.VMEM((8, E), f32)


def my_place():
    me = lax.axis_index("seq")
    return me // (2 * L), lax.rem(me // 2, L), lax.rem(me, 2)


def by_core(kernel):
    def whole(*refs):
        _, _, core = my_place()
        for c in range(2):
            pl.when(core == c)(functools.partial(kernel, c * HALF, (1 - c) * HALF, *refs))

    return whole


def far(*arrays):
    return tuple(pltpu.with_memory_space_constraint(a, pltpu.HBM) for a in arrays)


def near(*arrays):
    return tuple(pltpu.with_memory_space_constraint(a, pltpu.VMEM) for a in arrays)


def rows(step):
    if isinstance(step, int):
        return slice(step * C, (step + 1) * C)
    return pl.ds(pl.multiple_of(step * C, C), C)


def by_chunk(kernel):
    def whole(*refs):
        for step in range(NC):
            kernel(step, *refs)

    return whole


def mm_lower(a, b):
    return jnp.concatenate([mm(a[:B, :B], b[:B]), mm(a[B:], b)], axis=0)


def mm_upper(a, b):
    return jnp.concatenate([mm(a[:B], b), mm(a[B:, B:], b[B:])], axis=0)


def kv_other_kernel(mine, other, k_hbm, v_hbm, kh_ref, vh_ref, o_ref, k_buf, v_buf, sems):
    copies = []
    for i in range(NB):
        at = pl.ds(i * B, B)
        for n, (src, dst) in enumerate(((k_hbm, k_buf), (v_hbm, v_buf))):
            copies.append(pltpu.make_async_copy(src.at[at], dst.at[at], sems.at[i, n]))
            copies[-1].start()
    for i in range(NB):
        at = slice(i * B, (i + 1) * B)
        copies[2 * i].wait()
        kh_ref[:, at] = jnp.swapaxes(k_buf[at], 0, 1)
        copies[2 * i + 1].wait()
        vh_ref[:, at] = jnp.swapaxes(v_buf[at], 0, 1)
    for j in range(HALF):
        o_ref[j] = mm_tn(kh_ref[other + j], vh_ref[other + j])


def kv_other(keys, values):
    return pl.pallas_call(
        by_core(kv_other_kernel),
        in_specs=[AWAY, AWAY],
        out_specs=[HERE] * 3,
        out_shape=[MAJOR] * 2 + [pltpu.VMEM((HALF, E, E), f32)],
        scratch_shapes=[
            pltpu.VMEM((T, HL, E), bf16),
            pltpu.VMEM((T, HL, E), bf16),
            pltpu.SemaphoreType.DMA((NB, 2)),
        ],
        compiler_params=params(24),
        cost_estimate=cost(T * HL * E * E, 7 * MIB),
        name="kv_other",
    )(*far(keys, values))


def kv_mine_kernel(mine, other, k_ref, v_ref, o_ref):
    for j in range(HALF):
        o_ref[j] = mm_tn(k_ref[mine + j], v_ref[mine + j])


def kv_mine(kh, vh):
    return pl.pallas_call(
        by_core(kv_mine_kernel),
        in_specs=[HERE] * 2,
        out_specs=HERE,
        out_shape=pltpu.VMEM((HALF, E, E), f32),
        compiler_params=params(4),
        cost_estimate=cost(T * HL * E * E, MIB),
        name="kv_mine",
    )(*near(kh, vh))


def pair_kernel(first, m_ref, r_ref, *outs):
    _, z, core = my_place()
    for out, k in zip(outs, ZSTEPS):
        at = lax.rem(z + k, L)
        out[...] = m_ref[at] + r_ref[at]
    outs[L][...] = jnp.where(core == first, m_ref[...], r_ref[...])


def pair(mine, got, first):
    return pl.pallas_call(
        functools.partial(pair_kernel, first),
        in_specs=[HERE] * 2,
        out_specs=[HERE] * (L + 1),
        out_shape=[QUARTER] * L + [QUARTERS],
        compiler_params=params(2),
        cost_estimate=cost(HALF * E * E, 2 * MIB),
        name="pair",
    )(*near(mine, got))


def row_kernel(backward, *refs):
    parts, (_, e_ref, t_ref, buf) = refs[:L], refs[L:]
    _, z, _ = my_place()
    for part, k in zip(parts, ZSTEPS):
        buf[lax.rem(z + L - k, L)] = part[...]
    total = jnp.zeros_like(t_ref)
    for i in reversed(range(L)) if backward else range(L):
        e_ref[i] = total
        total = total + buf[i]
    t_ref[...] = total


def row_sums(parts, order, backward):
    return pl.pallas_call(
        functools.partial(row_kernel, backward),
        in_specs=[HERE] * (L + 1),
        out_specs=[HERE] * 2,
        out_shape=[QUARTERS, QUARTER],
        scratch_shapes=[QUARTERS],
        compiler_params=params(2),
        cost_estimate=cost(HALF * E * E, MIB),
        name="row_sums",
    )(*near(*parts, order))


def prior_kernel(e_ref, u1, u2, u3, x_ref, _, *outs):
    y, z, _ = my_place()
    total = x_ref[...]
    for k, u in zip(YSTEPS, (u1, u2, u3)):
        total = total + jnp.where(k <= y, u[...], 0.0)
    for out, k in zip(outs, ZSTEPS):
        out[...] = total + e_ref[lax.rem(z + k, L)]


def prior_sums(inrow, others, start, order):
    return pl.pallas_call(
        prior_kernel,
        in_specs=[HERE] * (L + 2),
        out_specs=[HERE] * L,
        out_shape=[QUARTER] * L,
        compiler_params=params(2),
        cost_estimate=cost(HALF * E * E, MIB),
        name="prior_sums",
    )(*near(inrow, *others, start, order))


def later_kernel(e_ref, t_ref, u1, u2, u3, _, *refs):
    outs, (keep_ref, send_ref, buf) = refs[:L], refs[L:]
    y, z, core = my_place()
    total = jnp.zeros_like(t_ref)
    for k, u in zip(YSTEPS, (u1, u2, u3)):
        total = total + jnp.where(k > y, u[...], 0.0)
    for out, k in zip(outs, ZSTEPS):
        out[...] = total + e_ref[lax.rem(z + k, L)]
    buf[...] = (t_ref[...] + u1[...] + u2[...] + u3[...]).reshape(buf.shape)
    low = lax.broadcasted_iota(jnp.int32, (8, E), 0) < 4
    for j in range(0, HALF, 2):
        a = buf[y, 8 * j : 8 * j + 8]
        b = buf[y, 8 * j + 8 : 8 * j + 16]
        even = jnp.where(low, a, pltpu.roll(b, 4, 0))
        odd = jnp.where(low, pltpu.roll(a, 4, 0), b)
        keep_ref[4 * j : 4 * j + 8] = jnp.where(core == 0, even, odd)
        send_ref[4 * j : 4 * j + 8] = jnp.where(core == 0, odd, even)


def later_sums(inrow, total, others, order):
    return pl.pallas_call(
        later_kernel,
        in_specs=[HERE] * (L + 2),
        out_specs=[HERE] * (L + 2),
        out_shape=[QUARTER] * L + [pltpu.VMEM((HALF * L, E), f32)] * 2,
        scratch_shapes=[pltpu.VMEM((L, HALF * 8, E), f32)],
        compiler_params=params(2),
        cost_estimate=cost(HALF * E * E, MIB),
        name="later_sums",
    )(*near(inrow, total, *others, order))


def split_kernel(first, *refs):
    parts, (x_ref, _, own_ref, send_ref) = refs[:L], refs[L:]
    _, z, core = my_place()
    for part, k in zip(parts, ZSTEPS):
        at = lax.rem(z + L - k, L)
        scan = part[...]
        more = scan + x_ref[at]
        own_ref[at] = jnp.where(core == first, scan, more)
        send_ref[at] = jnp.where(core == first, more, scan)


def split(parts, extra, order, first):
    return pl.pallas_call(
        functools.partial(split_kernel, first),
        in_specs=[HERE] * (L + 2),
        out_specs=[HERE] * 2,
        out_shape=[QUARTERS] * 2,
        compiler_params=params(2),
        cost_estimate=cost(HALF * E * E, 2 * MIB),
        name="split",
    )(*near(*parts, extra, order))


def local_kernel(q_hbm, k_ref, v_ref, x_hbm, _, qh_ref, loc_ref, x_ref, mark_ref, q_buf, sems):
    _, z, core = my_place()
    copies = [pltpu.make_async_copy(x_hbm.at[core * L + z], x_ref, sems.at[NC])]
    for i in range(NC):
        at = pl.ds(i * C, C)
        copies.append(pltpu.make_async_copy(q_hbm.at[at], q_buf.at[at], sems.at[i]))
    for copy in copies:
        copy.start()
    mark_ref[...] = jnp.zeros_like(mark_ref)
    for h in range(HL):
        total = mm_tn(k_ref[h, :C], v_ref[h, :C])
        loc_ref[0, h] = jnp.zeros((E, E), bf16)
        loc_ref[1, h] = total.astype(bf16)
        loc_ref[2, h] = (total + mm_tn(k_ref[h, C : 2 * C], v_ref[h, C : 2 * C])).astype(bf16)
    for i in range(NC):
        at = slice(i * C, (i + 1) * C)
        copies[i + 1].wait()
        qh_ref[:, at] = jnp.swapaxes(q_buf[at], 0, 1)
    copies[0].wait()


def local_states(queries, kh, vh, start, order):
    return pl.pallas_call(
        local_kernel,
        in_specs=[AWAY] + [HERE] * 2 + [AWAY, HERE],
        out_specs=[HERE] * 4,
        out_shape=[MAJOR, STATES, QUARTER, MARK],
        scratch_shapes=[pltpu.VMEM((T, HL, E), bf16), pltpu.SemaphoreType.DMA((NC + 1,))],
        compiler_params=params(12),
        cost_estimate=cost(2 * T * HL * E * E, 12 * MIB),
        name="local_states",
    )(*far(queries), *near(kh, vh), *far(start), *near(order))


def inner_kernel(step, q_ref, k_ref, v_ref, loc_ref, _, att_ref, mark_ref, qk_ref):
    at = rows(step)
    mask = causal()
    mark_ref[...] = jnp.zeros_like(mark_ref)
    for h in range(HL):
        qk_ref[h] = jnp.where(mask, mm_nt(q_ref[h, at], k_ref[h, at]), 0.0).astype(bf16)
    for h in range(HL):
        att = mm_lower(qk_ref[h], v_ref[h, at])
        if step > 0:
            att = att + mm(q_ref[h, at], loc_ref[step, h])
        att_ref[h, at] = att.astype(bf16)


def inner_part(qh, kh, vh, loc, order):
    return pl.pallas_call(
        by_chunk(inner_kernel),
        in_specs=[HERE] * 5,
        out_specs=[HERE] * 2,
        out_shape=[MAJOR, MARK],
        scratch_shapes=[pltpu.VMEM((HL, C, C), bf16)],
        compiler_params=params(8),
        cost_estimate=cost(2 * T * HL * (2 * C * E + E * E), 16 * MIB),
        name="inner_part",
    )(*near(qh, kh, vh, loc, order))


def square_kernel(g_hbm, q_ref, k_ref, _, gh_ref, kq_ref, mark_ref, g_buf, sems):
    copies = []
    for i in range(NC):
        at = pl.ds(i * C, C)
        copies.append(pltpu.make_async_copy(g_hbm.at[at], g_buf.at[at], sems.at[i]))
        copies[-1].start()
    mask = causal(later=True)
    mark_ref[...] = jnp.zeros_like(mark_ref)
    for i in range(NC):
        at = slice(i * C, (i + 1) * C)
        for h in range(HL):
            kq_ref[h, at] = jnp.where(mask, mm_nt(k_ref[h, at], q_ref[h, at]), 0.0).astype(bf16)
    for i in range(NC):
        at = slice(i * C, (i + 1) * C)
        copies[i].wait()
        gh_ref[:, at] = jnp.swapaxes(g_buf[at], 0, 1)


def square_part(out_grad, qh, kh, order):
    return pl.pallas_call(
        square_kernel,
        in_specs=[AWAY] + [HERE] * 3,
        out_specs=[HERE] * 3,
        out_shape=[MAJOR, SQUARES, MARK],
        scratch_shapes=[pltpu.VMEM((T, HL, E), bf16), pltpu.SemaphoreType.DMA((NC,))],
        compiler_params=params(8),
        cost_estimate=cost(2 * T * HL * C * E, 12 * MIB),
        name="square_part",
    )(*far(out_grad), *near(qh, kh, order))


def stats_half(first, h, state, refs, sq, pr, at):
    q_ref, g_ref, a_ref, gain_ref, att_ref = refs
    for j in range(HALF):
        att = a_ref[h + j, at].astype(f32) + mm(q_ref[h + j, at], state[j])
        att_ref[h + j, at] = att
        up = gain_ref[pl.ds(h + j, 1), :] * g_ref[h + j, at].astype(f32)
        sq = sq + att * att
        pr = pr + up * att
    return sq, pr


def stats_own_kernel(step, mine, other, q_ref, g_ref, a_ref, own_ref, gain_ref, att_ref, sb_ref, sum_ref):
    at = rows(step)

    @pl.when(step == 0)
    def _():
        sb_ref[pl.ds(mine, HALF)] = own_ref[...].astype(bf16)

    state = [sb_ref[mine + j] for j in range(HALF)]
    zero = jnp.zeros((C, E), f32)
    refs = (q_ref, g_ref, a_ref, gain_ref, att_ref)
    sum_ref[0, at], sum_ref[1, at] = stats_half(0, mine, state, refs, zero, zero, at)


def stats_got_kernel(
    step, mine, other, q_ref, g_ref, a_ref, got_ref, gain_ref, sum_ref, _, __, att_ref, sb_ref, o_ref
):
    at = rows(step)

    @pl.when(step == 0)
    def _():
        sb_ref[pl.ds(other, HALF)] = got_ref[...].astype(bf16)

    state = [sb_ref[other + j] for j in range(HALF)]
    refs = (q_ref, g_ref, a_ref, gain_ref, att_ref)
    sq, pr = stats_half(1, other, state, refs, sum_ref[0, at], sum_ref[1, at], at)
    o_ref[step, 0:1, :] = jnp.sum(sq.T, axis=0, keepdims=True)
    o_ref[step, 1:2, :] = jnp.sum(pr.T, axis=0, keepdims=True)


ATTENDED = pltpu.VMEM((HL, T, E), f32)
STATE = pltpu.VMEM((HL, E, E), bf16)


def stats_own(qh, gh, part, own, gain):
    return pl.pallas_call(
        by_core(by_chunk(stats_own_kernel)),
        in_specs=[HERE] * 5,
        out_specs=[HERE] * 3,
        out_shape=[ATTENDED, STATE, pltpu.VMEM((2, T, E), f32)],
        compiler_params=params(6),
        cost_estimate=cost(T * HL * E * E, 5 * MIB),
        name="stats_own",
    )(*near(qh, gh, part, own, gain))


def stats_got(qh, gh, part, got, gain, sums, att, state):
    return pl.pallas_call(
        by_core(by_chunk(stats_got_kernel)),
        in_specs=[HERE] * 8,
        out_specs=[HERE] * 3,
        out_shape=[ATTENDED, STATE, pltpu.VMEM((NC, 2, C), f32)],
        input_output_aliases={6: 0, 7: 1},
        compiler_params=params(6),
        cost_estimate=cost(T * HL * E * E, 5 * MIB),
        name="stats_got",
    )(*near(qh, gh, part, got, gain, sums, att, state))


def scales(sums, step):
    sums = sums[step]
    rms = jnp.sqrt(sums[0:1, :] / WIDTH + epsilon)
    a = 1.0 / rms
    b = sums[1:2, :] / (WIDTH * rms * rms) * a
    a = jnp.broadcast_to(a, (E, C)).T
    b = jnp.broadcast_to(b, (E, C)).T
    return a, b


def pre_kernel(step, mine, other, q_ref, g_ref, a_ref, gain_ref, s_ref, *refs, own):
    p_ref, wl_ref, w_ref, acc = refs[-4:]
    chunk = NC - 1 - step
    at = rows(chunk)
    first = mine if own else other

    @pl.when(step == 0)
    def _():
        acc[...] = jnp.zeros_like(acc)

    a, b = scales(s_ref, chunk)
    wl_ref[chunk, pl.ds(first, HALF)] = acc[...].astype(bf16)
    for j in range(HALF):
        h = first + j
        up = gain_ref[pl.ds(h, 1), :] * g_ref[h, at].astype(f32)
        p = (up * a - a_ref[h, at] * b).astype(bf16)
        p_ref[h, at] = p
        acc[j] += mm_tn(q_ref[h, at], p)

    @pl.when(step == NC - 1)
    def _():
        for j in range(HALF):
            x = acc[j]
            for n in range(L * L):
                to = slice(64 * (n // L) + 8 * j, 64 * (n // L) + 8 * j + 8)
                w_ref[n % L, to, :] = x[8 * n : 8 * n + 8]


def pre_part(qh, gh, att, gain, sums, *half_done):
    own = len(half_done) > 0
    return pl.pallas_call(
        by_core(by_chunk(functools.partial(pre_kernel, own=own))),
        in_specs=[HERE] * (5 + len(half_done)),
        out_specs=[HERE] * 3,
        out_shape=[MAJOR, STATES, QUARTERS],
        input_output_aliases={5: 0, 6: 1} if own else {},
        scratch_shapes=[pltpu.VMEM((HALF, E, E), f32)],
        compiler_params=params(6),
        cost_estimate=cost(T * HL * E * E, 8 * MIB),
        name="pre_own" if own else "pre_other",
    )(*near(qh, gh, att, gain, *sums, *half_done))


def query_kernel(step, k_ref, v_ref, p_ref, s_ref, loc_ref, _, qg_ref, mark_ref, gv_ref, sum_ref):
    at = rows(step)
    mask = causal()
    mark_ref[...] = jnp.zeros_like(mark_ref)
    for h in range(HL):
        gv_ref[h] = jnp.where(mask, mm_nt(p_ref[h, at], v_ref[h, at]), 0.0).astype(bf16)
    for h in range(HL):
        p = p_ref[h, at]
        sum_ref[h] = mm_nt(
            jnp.concatenate([p, p], axis=1),
            jnp.concatenate([s_ref[h], loc_ref[step, h]], axis=1),
        )
    for h in range(HL):
        qg_ref[h, at] = (sum_ref[h] + mm_lower(gv_ref[h], k_ref[h, at])).astype(bf16)


def query_part(kh, vh, pre, state, loc, order):
    return pl.pallas_call(
        by_chunk(query_kernel),
        in_specs=[HERE] * 6,
        out_specs=[HERE] * 2,
        out_shape=[MAJOR, MARK],
        scratch_shapes=[pltpu.VMEM((HL, C, C), bf16), pltpu.VMEM((HL, C, E), f32)],
        compiler_params=params(8),
        cost_estimate=cost(2 * T * HL * (2 * C * E + 2 * E * E), 16 * MIB),
        name="query_part",
    )(*near(kh, vh, pre, state, loc, order))


def key_kernel(step, q_ref, v_ref, p_ref, wl_ref, _, kg_ref, mark_ref, vp_ref, sum_ref):
    at = rows(step)
    mask = causal(later=True)
    mark_ref[...] = jnp.zeros_like(mark_ref)
    for h in range(HL):
        vp_ref[h] = jnp.where(mask, mm_nt(v_ref[h, at], p_ref[h, at]), 0.0).astype(bf16)
    if step < NC - 1:
        for h in range(HL):
            sum_ref[h] = mm_nt(v_ref[h, at], wl_ref[step, h])
    for h in range(HL):
        part = mm_upper(vp_ref[h], q_ref[h, at])
        if step < NC - 1:
            part = part + sum_ref[h]
        kg_ref[h, at] = part.astype(bf16)


def key_part(qh, vh, pre, wloc, order):
    return pl.pallas_call(
        by_chunk(key_kernel),
        in_specs=[HERE] * 5,
        out_specs=[HERE] * 2,
        out_shape=[MAJOR, MARK],
        scratch_shapes=[pltpu.VMEM((HL, C, C), bf16), pltpu.VMEM((HL, C, E), f32)],
        compiler_params=params(8),
        cost_estimate=cost(2 * T * HL * (2 * C * E + E * E), 16 * MIB),
        name="key_part",
    )(*near(qh, vh, pre, wloc, order))


def value_kernel(
    k_ref, p_ref, kq_ref, wl_ref, a_ref, qh_ref, gain_ref, s_ref, _, n_ref, qg_ref, vg_ref, mark_ref
):
    step = pl.program_id(0)
    at = rows(step)
    mark_ref[...] = jnp.zeros_like(mark_ref)
    a, _ = scales(s_ref, step)
    normed = [(gain_ref[h : h + 1, :] * a_ref[h, at] * a).astype(bf16) for h in range(HL)]
    n_ref[...] = jnp.swapaxes(jnp.stack(normed), 0, 1)
    qg_ref[...] = jnp.swapaxes(qh_ref[:, at], 0, 1)
    for h in range(HL):
        part = mm_upper(kq_ref[h, at], p_ref[h, at]) + mm(k_ref[h, at], wl_ref[step, h])
        vg_ref[h, at] = part.astype(bf16)


def value_part(kh, pre, kq, wloc, att, grad, gain, sums, order):
    return pl.pallas_call(
        value_kernel,
        grid=(NC,),
        in_specs=[HERE] * 9,
        out_specs=[TOK, TOK, HERE, HERE],
        out_shape=[TOKENS, TOKENS, MAJOR, MARK],
        compiler_params=params(14),
        cost_estimate=cost(2 * T * HL * (C * E + E * E), 20 * MIB),
        name="value_part",
    )(*near(kh, pre, kq, wloc, att, grad, gain, *sums, order))


def final_half(first, l_ref, k_ref, v_ref, kg_ref, vg_ref, at):
    for j in range(HALF):
        h = first + j
        kg_ref[h, at] = (kg_ref[h, at].astype(f32) + mm_nt(v_ref[h, at], l_ref[j])).astype(bf16)
    for j in range(HALF):
        h = first + j
        vg_ref[h, at] = (vg_ref[h, at].astype(f32) + mm(k_ref[h, at], l_ref[j])).astype(bf16)


def in_order(l_ref, x_ref):
    for j in range(HALF):
        parts = []
        for n in range(L * L):
            first = 64 * (n // L) + 8 * j
            parts.append(x_ref[n % L, first : first + 8, :])
        l_ref[j] = jnp.concatenate(parts, axis=0).astype(bf16)


def final_own_kernel(step, mine, other, k_ref, v_ref, own_ref, _, __, kg_ref, vg_ref, l_ref):

    @pl.when(step == 0)
    def _():
        in_order(l_ref, own_ref)

    final_half(mine, l_ref, k_ref, v_ref, kg_ref, vg_ref, rows(step))


def final_own(kh, vh, own, kpart, vpart):
    return pl.pallas_call(
        by_core(by_chunk(final_own_kernel)),
        in_specs=[HERE] * 5,
        out_specs=[HERE] * 2,
        out_shape=[MAJOR] * 2,
        input_output_aliases={3: 0, 4: 1},
        scratch_shapes=[pltpu.VMEM((HALF, E, E), bf16)],
        compiler_params=params(4),
        cost_estimate=cost(2 * T * HL * E * E, 8 * MIB),
        name="final_own",
    )(*near(kh, vh, own, kpart, vpart))


def final_got_kernel(
    mine, other, k_ref, v_ref, got_ref, kp_ref, vp_ref, mine_ref, theirs_ref, kg_ref, vg_ref, e_ref, l_ref
):
    step = pl.program_id(0)
    at = rows(step)

    @pl.when(step == 0)
    def _():
        in_order(l_ref, got_ref)
        e_ref[mine * L : (mine + HALF) * L] = mine_ref[...]
        e_ref[other * L : (other + HALF) * L] = theirs_ref[...]

    final_half(other, l_ref, k_ref, v_ref, kp_ref, vp_ref, at)
    kg_ref[...] = jnp.swapaxes(kp_ref[:, at], 0, 1)
    vg_ref[...] = jnp.swapaxes(vp_ref[:, at], 0, 1)


def final_got(kh, vh, got, kpart, vpart, mine, theirs):
    return pl.pallas_call(
        by_core(final_got_kernel),
        grid=(NC,),
        in_specs=[HERE] * 7,
        out_specs=[TOK] * 2 + [HERE],
        out_shape=[TOKENS] * 2 + [jax.ShapeDtypeStruct((HL * L, E), f32)],
        scratch_shapes=[pltpu.VMEM((HALF, E, E), bf16)],
        compiler_params=params(14),
        cost_estimate=cost(2 * T * HL * E * E, 15 * MIB),
        name="final_got",
    )(*near(kh, vh, got, kpart, vpart, mine, theirs))


def along(x, move):
    def seq(y, z, core):
        return (y * L + z) * 2 + core

    places = [(y, z, core) for y in range(L) for z in range(L) for core in range(2)]
    return lax.ppermute(x, "seq", [(seq(*p), seq(*move(*p))) for p in places])


def across_cores(x):
    return along(x, lambda y, z, core: (y, z, 1 - core))


def across_z(parts):
    return list(parts[:1]) + [
        along(x, lambda y, z, core: (y, (z + k) % L, core)) for x, k in zip(parts[1:], ZSTEPS[1:])
    ]


def across_y(x):
    return [along(x, lambda y, z, core: ((y + k) % L, z, core)) for k in YSTEPS]


def add_kernel(a_ref, b_ref, o_ref):
    o_ref[...] = a_ref[...] + b_ref[...]


def across_heads(x):
    for partner in (lambda i: i ^ 1, lambda i: X - 1 - i):
        got = lax.ppermute(x, "head", [(i, partner(i)) for i in range(X)])
        x = pl.pallas_call(
            add_kernel,
            in_specs=[HERE] * 2,
            out_specs=HERE,
            out_shape=pltpu.VMEM((NC, 2, C), f32),
            compiler_params=params(2),
            name="add",
        )(*near(x, got))
    return [x]


def body(queries, keys, values, out_grad, gain, entry_state):
    rows_of = HALF * E // L
    start = entry_state.reshape(2 * L, rows_of, E)
    kh, vh, other = kv_other(keys, values)
    got = across_cores(other.reshape(L, rows_of, E))
    *parts, extra = pair(kv_mine(kh, vh).reshape(L, rows_of, E), got, 0)
    near_row = across_z(parts)
    qh, loc, start, mark = local_states(queries, kh, vh, start, parts[0])
    inrow, total = row_sums(near_row, mark, False)
    others = across_y(total)
    part, mark = inner_part(qh, kh, vh, loc, total)
    parts = prior_sums(inrow, others, start, mark)
    scan = across_z(parts)
    gh, kq, mark = square_part(out_grad, qh, kh, parts[0])
    own, other = split(scan, extra, mark, 0)
    got = across_cores(other)
    att, state, sums = stats_own(qh, gh, part, own.reshape(HALF, E, E), gain)
    got = got.reshape(HALF, E, E)
    att, state, sums = stats_got(qh, gh, part, got, gain, sums, att, state)
    sums = across_heads(sums)
    pre, wloc, other = pre_part(qh, gh, att, gain, sums)
    got = across_cores(other)
    pre, wloc, mine = pre_part(qh, gh, att, gain, sums, pre, wloc)
    *parts, extra = pair(mine, got, 1)
    near_row = across_z(parts)
    grad, mark = query_part(kh, vh, pre, state, loc, parts[0])
    inrow, total = row_sums(near_row, mark, True)
    others = across_y(total)
    kpart, mark = key_part(qh, vh, pre, wloc, total)
    *parts, mine, theirs = later_sums(inrow, total, others, mark)
    scan = across_z(parts)
    theirs = across_cores(theirs)
    normed, query_grad, vpart, mark = value_part(
        kh, pre, kq, wloc, att, grad, gain, sums, parts[0]
    )
    own, other = split(scan, extra, mark, 1)
    got = across_cores(other)
    kpart, vpart = final_own(kh, vh, own, kpart, vpart)
    key_grad, value_grad, entry_grad = final_got(kh, vh, got, kpart, vpart, mine, theirs)
    return normed, query_grad, key_grad, value_grad, entry_grad.reshape(HL, L, E)


def solution(mesh):
    tok = P("seq", "head", None)
    return jax.shard_map(
        body,
        mesh=mesh,
        in_specs=(tok, tok, tok, tok, P("head", None), P("head", None, None)),
        out_specs=(tok, tok, tok, tok, P("head", "seq", None)),
        check_vma=False,
    )
```

```python
import functools

import jax
import jax.numpy as jnp
from jax import lax
from jax.experimental import pallas as pl
from jax.experimental.pallas import tpu as pltpu
from jax.sharding import PartitionSpec as P

H = 64
E = 128
T = 768
HL = 16
C = 256
NC = T // C
B = 128
NB = T // B
ZSTEPS = (0, 2, 1, 3)
YSTEPS = (1, 3, 2)
N = 32
L = 4
HALF = HL // 2
X = 4
WIDTH = H * E
epsilon = 1e-06
f32 = jnp.float32
bf16 = jnp.bfloat16
MIB = 1 << 20


def mm(a, b):
    return lax.dot_general(a, b, (((1,), (0,)), ((), ())), preferred_element_type=f32)


def mm_nt(a, b):
    return lax.dot_general(a, b, (((1,), (1,)), ((), ())), preferred_element_type=f32)


def mm_tn(a, b):
    return lax.dot_general(a, b, (((0,), (0,)), ((), ())), preferred_element_type=f32)


def causal(later=False):
    row = lax.broadcasted_iota(jnp.int32, (C, C), 0)
    col = lax.broadcasted_iota(jnp.int32, (C, C), 1)
    return row <= col if later else col <= row


def heads_first(ref):
    return jnp.swapaxes(ref[...], 0, 1)


def params(vmem=24):
    return pltpu.CompilerParams(vmem_limit_bytes=vmem * MIB)


def cost(flops, moved):
    return pl.CostEstimate(flops=flops, bytes_accessed=moved, transcendentals=0)


HERE = pl.BlockSpec(memory_space=pltpu.VMEM)
AWAY = pl.BlockSpec(memory_space=pl.ANY)
TOK = pl.BlockSpec((C, HL, E), lambda i: (i, 0, 0))
MAJOR = pltpu.VMEM((HL, T, E), bf16)
SQUARES = pltpu.VMEM((HL, T, C), bf16)
STATES = pltpu.VMEM((NC, HL, E, E), bf16)
TOKENS = pltpu.HBM((T, HL, E), bf16)
QUARTER = pltpu.VMEM((HALF * E // L, E), f32)
QUARTERS = pltpu.VMEM((L, HALF * E // L, E), f32)
MARK = pltpu.VMEM((8, E), f32)


def my_place():
    me = lax.axis_index("seq")
    return me // (2 * L), lax.rem(me // 2, L), lax.rem(me, 2)


def by_core(kernel):
    def whole(*refs):
        _, _, core = my_place()
        for c in range(2):
            pl.when(core == c)(functools.partial(kernel, c * HALF, (1 - c) * HALF, *refs))

    return whole


def far(*arrays):
    return tuple(pltpu.with_memory_space_constraint(a, pltpu.HBM) for a in arrays)


def near(*arrays):
    return tuple(pltpu.with_memory_space_constraint(a, pltpu.VMEM) for a in arrays)


def rows(step):
    if isinstance(step, int):
        return slice(step * C, (step + 1) * C)
    return pl.ds(pl.multiple_of(step * C, C), C)


def by_chunk(kernel):
    def whole(*refs):
        for step in range(NC):
            kernel(step, *refs)

    return whole


def mm_lower(a, b):
    return jnp.concatenate([mm(a[:B, :B], b[:B]), mm(a[B:], b)], axis=0)


def mm_upper(a, b):
    return jnp.concatenate([mm(a[:B], b), mm(a[B:, B:], b[B:])], axis=0)


def kv_other_kernel(mine, other, k_hbm, v_hbm, kh_ref, vh_ref, o_ref, k_buf, v_buf, sems):
    copies = []
    for i in range(NB):
        at = pl.ds(i * B, B)
        for n, (src, dst) in enumerate(((k_hbm, k_buf), (v_hbm, v_buf))):
            copies.append(pltpu.make_async_copy(src.at[at], dst.at[at], sems.at[i, n]))
            copies[-1].start()
    for i in range(NB):
        at = slice(i * B, (i + 1) * B)
        copies[2 * i].wait()
        kh_ref[:, at] = jnp.swapaxes(k_buf[at], 0, 1)
        copies[2 * i + 1].wait()
        vh_ref[:, at] = jnp.swapaxes(v_buf[at], 0, 1)
    for j in range(HALF):
        o_ref[j] = mm_tn(kh_ref[other + j], vh_ref[other + j])


def kv_other(keys, values):
    return pl.pallas_call(
        by_core(kv_other_kernel),
        in_specs=[AWAY, AWAY],
        out_specs=[HERE] * 3,
        out_shape=[MAJOR] * 2 + [pltpu.VMEM((HALF, E, E), f32)],
        scratch_shapes=[
            pltpu.VMEM((T, HL, E), bf16),
            pltpu.VMEM((T, HL, E), bf16),
            pltpu.SemaphoreType.DMA((NB, 2)),
        ],
        compiler_params=params(24),
        cost_estimate=cost(T * HL * E * E, 7 * MIB),
        name="kv_other",
    )(*far(keys, values))


def kv_mine_kernel(mine, other, k_ref, v_ref, o_ref):
    for j in range(HALF):
        o_ref[j] = mm_tn(k_ref[mine + j], v_ref[mine + j])


def kv_mine(kh, vh):
    return pl.pallas_call(
        by_core(kv_mine_kernel),
        in_specs=[HERE] * 2,
        out_specs=HERE,
        out_shape=pltpu.VMEM((HALF, E, E), f32),
        compiler_params=params(4),
        cost_estimate=cost(T * HL * E * E, MIB),
        name="kv_mine",
    )(*near(kh, vh))


def pair_kernel(first, m_ref, r_ref, *outs):
    _, z, core = my_place()
    for out, k in zip(outs, ZSTEPS):
        at = lax.rem(z + k, L)
        out[...] = m_ref[at] + r_ref[at]
    outs[L][...] = jnp.where(core == first, m_ref[...], r_ref[...])


def pair(mine, got, first):
    return pl.pallas_call(
        functools.partial(pair_kernel, first),
        in_specs=[HERE] * 2,
        out_specs=[HERE] * (L + 1),
        out_shape=[QUARTER] * L + [QUARTERS],
        compiler_params=params(2),
        cost_estimate=cost(HALF * E * E, 2 * MIB),
        name="pair",
    )(*near(mine, got))


def row_kernel(backward, *refs):
    parts, (_, e_ref, t_ref, buf) = refs[:L], refs[L:]
    _, z, _ = my_place()
    for part, k in zip(parts, ZSTEPS):
        buf[lax.rem(z + L - k, L)] = part[...]
    total = jnp.zeros_like(t_ref)
    for i in reversed(range(L)) if backward else range(L):
        e_ref[i] = total
        total = total + buf[i]
    t_ref[...] = total


def row_sums(parts, order, backward):
    return pl.pallas_call(
        functools.partial(row_kernel, backward),
        in_specs=[HERE] * (L + 1),
        out_specs=[HERE] * 2,
        out_shape=[QUARTERS, QUARTER],
        scratch_shapes=[QUARTERS],
        compiler_params=params(2),
        cost_estimate=cost(HALF * E * E, MIB),
        name="row_sums",
    )(*near(*parts, order))


def prior_kernel(e_ref, u1, u2, u3, x_ref, _, *outs):
    y, z, _ = my_place()
    total = x_ref[...]
    for k, u in zip(YSTEPS, (u1, u2, u3)):
        total = total + jnp.where(k <= y, u[...], 0.0)
    for out, k in zip(outs, ZSTEPS):
        out[...] = total + e_ref[lax.rem(z + k, L)]


def prior_sums(inrow, others, start, order):
    return pl.pallas_call(
        prior_kernel,
        in_specs=[HERE] * (L + 2),
        out_specs=[HERE] * L,
        out_shape=[QUARTER] * L,
        compiler_params=params(2),
        cost_estimate=cost(HALF * E * E, MIB),
        name="prior_sums",
    )(*near(inrow, *others, start, order))


def later_kernel(e_ref, t_ref, u1, u2, u3, _, *refs):
    outs, (keep_ref, send_ref, buf) = refs[:L], refs[L:]
    y, z, core = my_place()
    total = jnp.zeros_like(t_ref)
    for k, u in zip(YSTEPS, (u1, u2, u3)):
        total = total + jnp.where(k > y, u[...], 0.0)
    for out, k in zip(outs, ZSTEPS):
        out[...] = total + e_ref[lax.rem(z + k, L)]
    buf[...] = (t_ref[...] + u1[...] + u2[...] + u3[...]).reshape(buf.shape)
    low = lax.broadcasted_iota(jnp.int32, (8, E), 0) < 4
    for j in range(0, HALF, 2):
        a = buf[y, 8 * j : 8 * j + 8]
        b = buf[y, 8 * j + 8 : 8 * j + 16]
        even = jnp.where(low, a, pltpu.roll(b, 4, 0))
        odd = jnp.where(low, pltpu.roll(a, 4, 0), b)
        keep_ref[4 * j : 4 * j + 8] = jnp.where(core == 0, even, odd)
        send_ref[4 * j : 4 * j + 8] = jnp.where(core == 0, odd, even)


def later_sums(inrow, total, others, order):
    return pl.pallas_call(
        later_kernel,
        in_specs=[HERE] * (L + 2),
        out_specs=[HERE] * (L + 2),
        out_shape=[QUARTER] * L + [pltpu.VMEM((HALF * L, E), f32)] * 2,
        scratch_shapes=[pltpu.VMEM((L, HALF * 8, E), f32)],
        compiler_params=params(2),
        cost_estimate=cost(HALF * E * E, MIB),
        name="later_sums",
    )(*near(inrow, total, *others, order))


def split_kernel(first, *refs):
    parts, (x_ref, _, own_ref, send_ref) = refs[:L], refs[L:]
    _, z, core = my_place()
    for part, k in zip(parts, ZSTEPS):
        at = lax.rem(z + L - k, L)
        scan = part[...]
        more = scan + x_ref[at]
        own_ref[at] = jnp.where(core == first, scan, more)
        send_ref[at] = jnp.where(core == first, more, scan)


def split(parts, extra, order, first):
    return pl.pallas_call(
        functools.partial(split_kernel, first),
        in_specs=[HERE] * (L + 2),
        out_specs=[HERE] * 2,
        out_shape=[QUARTERS] * 2,
        compiler_params=params(2),
        cost_estimate=cost(HALF * E * E, 2 * MIB),
        name="split",
    )(*near(*parts, extra, order))


def local_kernel(q_hbm, k_ref, v_ref, x_hbm, _, qh_ref, loc_ref, x_ref, mark_ref, q_buf, sems):
    _, z, core = my_place()
    copies = [pltpu.make_async_copy(x_hbm.at[core * L + z], x_ref, sems.at[NC])]
    for i in range(NC):
        at = pl.ds(i * C, C)
        copies.append(pltpu.make_async_copy(q_hbm.at[at], q_buf.at[at], sems.at[i]))
    for copy in copies:
        copy.start()
    mark_ref[...] = jnp.zeros_like(mark_ref)
    for h in range(HL):
        total = mm_tn(k_ref[h, :C], v_ref[h, :C])
        loc_ref[0, h] = jnp.zeros((E, E), bf16)
        loc_ref[1, h] = total.astype(bf16)
        loc_ref[2, h] = (total + mm_tn(k_ref[h, C : 2 * C], v_ref[h, C : 2 * C])).astype(bf16)
    for i in range(NC):
        at = slice(i * C, (i + 1) * C)
        copies[i + 1].wait()
        qh_ref[:, at] = jnp.swapaxes(q_buf[at], 0, 1)
    copies[0].wait()


def local_states(queries, kh, vh, start, order):
    return pl.pallas_call(
        local_kernel,
        in_specs=[AWAY] + [HERE] * 2 + [AWAY, HERE],
        out_specs=[HERE] * 4,
        out_shape=[MAJOR, STATES, QUARTER, MARK],
        scratch_shapes=[pltpu.VMEM((T, HL, E), bf16), pltpu.SemaphoreType.DMA((NC + 1,))],
        compiler_params=params(12),
        cost_estimate=cost(2 * T * HL * E * E, 12 * MIB),
        name="local_states",
    )(*far(queries), *near(kh, vh), *far(start), *near(order))


def inner_kernel(step, q_ref, k_ref, v_ref, loc_ref, _, att_ref, mark_ref, qk_ref):
    at = rows(step)
    mask = causal()
    mark_ref[...] = jnp.zeros_like(mark_ref)
    for h in range(HL):
        qk_ref[h] = jnp.where(mask, mm_nt(q_ref[h, at], k_ref[h, at]), 0.0).astype(bf16)
    for h in range(HL):
        att = mm_lower(qk_ref[h], v_ref[h, at])
        if step > 0:
            att = att + mm(q_ref[h, at], loc_ref[step, h])
        att_ref[h, at] = att.astype(bf16)


def inner_part(qh, kh, vh, loc, order):
    return pl.pallas_call(
        by_chunk(inner_kernel),
        in_specs=[HERE] * 5,
        out_specs=[HERE] * 2,
        out_shape=[MAJOR, MARK],
        scratch_shapes=[pltpu.VMEM((HL, C, C), bf16)],
        compiler_params=params(8),
        cost_estimate=cost(2 * T * HL * (2 * C * E + E * E), 16 * MIB),
        name="inner_part",
    )(*near(qh, kh, vh, loc, order))


def square_kernel(g_hbm, q_ref, k_ref, _, gh_ref, kq_ref, mark_ref, g_buf, sems):
    copies = []
    for i in range(NC):
        at = pl.ds(i * C, C)
        copies.append(pltpu.make_async_copy(g_hbm.at[at], g_buf.at[at], sems.at[i]))
        copies[-1].start()
    mask = causal(later=True)
    mark_ref[...] = jnp.zeros_like(mark_ref)
    for i in range(NC):
        at = slice(i * C, (i + 1) * C)
        for h in range(HL):
            kq_ref[h, at] = jnp.where(mask, mm_nt(k_ref[h, at], q_ref[h, at]), 0.0).astype(bf16)
    for i in range(NC):
        at = slice(i * C, (i + 1) * C)
        copies[i].wait()
        gh_ref[:, at] = jnp.swapaxes(g_buf[at], 0, 1)


def square_part(out_grad, qh, kh, order):
    return pl.pallas_call(
        square_kernel,
        in_specs=[AWAY] + [HERE] * 3,
        out_specs=[HERE] * 3,
        out_shape=[MAJOR, SQUARES, MARK],
        scratch_shapes=[pltpu.VMEM((T, HL, E), bf16), pltpu.SemaphoreType.DMA((NC,))],
        compiler_params=params(8),
        cost_estimate=cost(2 * T * HL * C * E, 12 * MIB),
        name="square_part",
    )(*far(out_grad), *near(qh, kh, order))


def stats_half(first, h, state, refs, sq, pr, at):
    q_ref, g_ref, a_ref, gain_ref, att_ref = refs
    for j in range(HALF):
        att = a_ref[h + j, at].astype(f32) + mm(q_ref[h + j, at], state[j])
        att_ref[h + j, at] = att
        up = gain_ref[pl.ds(h + j, 1), :] * g_ref[h + j, at].astype(f32)
        sq = sq + att * att
        pr = pr + up * att
    return sq, pr


def stats_own_kernel(step, mine, other, q_ref, g_ref, a_ref, own_ref, gain_ref, att_ref, sb_ref, sum_ref):
    at = rows(step)

    @pl.when(step == 0)
    def _():
        sb_ref[pl.ds(mine, HALF)] = own_ref[...].astype(bf16)

    state = [sb_ref[mine + j] for j in range(HALF)]
    zero = jnp.zeros((C, E), f32)
    refs = (q_ref, g_ref, a_ref, gain_ref, att_ref)
    sum_ref[0, at], sum_ref[1, at] = stats_half(0, mine, state, refs, zero, zero, at)


def stats_got_kernel(
    step, mine, other, q_ref, g_ref, a_ref, got_ref, gain_ref, sum_ref, _, __, att_ref, sb_ref, o_ref
):
    at = rows(step)

    @pl.when(step == 0)
    def _():
        sb_ref[pl.ds(other, HALF)] = got_ref[...].astype(bf16)

    state = [sb_ref[other + j] for j in range(HALF)]
    refs = (q_ref, g_ref, a_ref, gain_ref, att_ref)
    sq, pr = stats_half(1, other, state, refs, sum_ref[0, at], sum_ref[1, at], at)
    o_ref[step, 0:1, :] = jnp.sum(sq.T, axis=0, keepdims=True)
    o_ref[step, 1:2, :] = jnp.sum(pr.T, axis=0, keepdims=True)


ATTENDED = pltpu.VMEM((HL, T, E), f32)
STATE = pltpu.VMEM((HL, E, E), bf16)


def stats_own(qh, gh, part, own, gain):
    return pl.pallas_call(
        by_core(by_chunk(stats_own_kernel)),
        in_specs=[HERE] * 5,
        out_specs=[HERE] * 3,
        out_shape=[ATTENDED, STATE, pltpu.VMEM((2, T, E), f32)],
        compiler_params=params(6),
        cost_estimate=cost(T * HL * E * E, 5 * MIB),
        name="stats_own",
    )(*near(qh, gh, part, own, gain))


def stats_got(qh, gh, part, got, gain, sums, att, state):
    return pl.pallas_call(
        by_core(by_chunk(stats_got_kernel)),
        in_specs=[HERE] * 8,
        out_specs=[HERE] * 3,
        out_shape=[ATTENDED, STATE, pltpu.VMEM((NC, 2, C), f32)],
        input_output_aliases={6: 0, 7: 1},
        compiler_params=params(6),
        cost_estimate=cost(T * HL * E * E, 5 * MIB),
        name="stats_got",
    )(*near(qh, gh, part, got, gain, sums, att, state))


def scales(sums, step):
    sums = sums[step]
    rms = jnp.sqrt(sums[0:1, :] / WIDTH + epsilon)
    a = 1.0 / rms
    b = sums[1:2, :] / (WIDTH * rms * rms) * a
    a = jnp.broadcast_to(a, (E, C)).T
    b = jnp.broadcast_to(b, (E, C)).T
    return a, b


def pre_kernel(step, mine, other, q_ref, g_ref, a_ref, gain_ref, s_ref, *refs, own):
    p_ref, wl_ref, w_ref, acc = refs[-4:]
    chunk = NC - 1 - step
    at = rows(chunk)
    first = mine if own else other

    @pl.when(step == 0)
    def _():
        acc[...] = jnp.zeros_like(acc)

    a, b = scales(s_ref, chunk)
    wl_ref[chunk, pl.ds(first, HALF)] = acc[...].astype(bf16)
    for j in range(HALF):
        h = first + j
        up = gain_ref[pl.ds(h, 1), :] * g_ref[h, at].astype(f32)
        p = (up * a - a_ref[h, at] * b).astype(bf16)
        p_ref[h, at] = p
        acc[j] += mm_tn(q_ref[h, at], p)

    @pl.when(step == NC - 1)
    def _():
        for j in range(HALF):
            x = acc[j]
            for n in range(L * L):
                to = slice(64 * (n // L) + 8 * j, 64 * (n // L) + 8 * j + 8)
                w_ref[n % L, to, :] = x[8 * n : 8 * n + 8]


def pre_part(qh, gh, att, gain, sums, *half_done):
    own = len(half_done) > 0
    return pl.pallas_call(
        by_core(by_chunk(functools.partial(pre_kernel, own=own))),
        in_specs=[HERE] * (5 + len(half_done)),
        out_specs=[HERE] * 3,
        out_shape=[MAJOR, STATES, QUARTERS],
        input_output_aliases={5: 0, 6: 1} if own else {},
        scratch_shapes=[pltpu.VMEM((HALF, E, E), f32)],
        compiler_params=params(6),
        cost_estimate=cost(T * HL * E * E, 8 * MIB),
        name="pre_own" if own else "pre_other",
    )(*near(qh, gh, att, gain, *sums, *half_done))


def query_kernel(step, k_ref, v_ref, p_ref, s_ref, loc_ref, _, qg_ref, mark_ref, gv_ref, sum_ref):
    at = rows(step)
    mask = causal()
    mark_ref[...] = jnp.zeros_like(mark_ref)
    for h in range(HL):
        gv_ref[h] = jnp.where(mask, mm_nt(p_ref[h, at], v_ref[h, at]), 0.0).astype(bf16)
    for h in range(HL):
        p = p_ref[h, at]
        sum_ref[h] = mm_nt(
            jnp.concatenate([p, p], axis=1),
            jnp.concatenate([s_ref[h], loc_ref[step, h]], axis=1),
        )
    for h in range(HL):
        qg_ref[h, at] = (sum_ref[h] + mm_lower(gv_ref[h], k_ref[h, at])).astype(bf16)


def query_part(kh, vh, pre, state, loc, order):
    return pl.pallas_call(
        by_chunk(query_kernel),
        in_specs=[HERE] * 6,
        out_specs=[HERE] * 2,
        out_shape=[MAJOR, MARK],
        scratch_shapes=[pltpu.VMEM((HL, C, C), bf16), pltpu.VMEM((HL, C, E), f32)],
        compiler_params=params(8),
        cost_estimate=cost(2 * T * HL * (2 * C * E + 2 * E * E), 16 * MIB),
        name="query_part",
    )(*near(kh, vh, pre, state, loc, order))


def key_kernel(step, q_ref, v_ref, p_ref, wl_ref, _, kg_ref, mark_ref, vp_ref, sum_ref):
    at = rows(step)
    mask = causal(later=True)
    mark_ref[...] = jnp.zeros_like(mark_ref)
    for h in range(HL):
        vp_ref[h] = jnp.where(mask, mm_nt(v_ref[h, at], p_ref[h, at]), 0.0).astype(bf16)
    if step < NC - 1:
        for h in range(HL):
            sum_ref[h] = mm_nt(v_ref[h, at], wl_ref[step, h])
    for h in range(HL):
        part = mm_upper(vp_ref[h], q_ref[h, at])
        if step < NC - 1:
            part = part + sum_ref[h]
        kg_ref[h, at] = part.astype(bf16)


def key_part(qh, vh, pre, wloc, order):
    return pl.pallas_call(
        by_chunk(key_kernel),
        in_specs=[HERE] * 5,
        out_specs=[HERE] * 2,
        out_shape=[MAJOR, MARK],
        scratch_shapes=[pltpu.VMEM((HL, C, C), bf16), pltpu.VMEM((HL, C, E), f32)],
        compiler_params=params(8),
        cost_estimate=cost(2 * T * HL * (2 * C * E + E * E), 16 * MIB),
        name="key_part",
    )(*near(qh, vh, pre, wloc, order))


def value_kernel(
    k_ref, p_ref, kq_ref, wl_ref, a_ref, qh_ref, gain_ref, s_ref, _, n_ref, qg_ref, vg_ref, mark_ref
):
    step = pl.program_id(0)
    at = rows(step)
    mark_ref[...] = jnp.zeros_like(mark_ref)
    a, _ = scales(s_ref, step)
    normed = [(gain_ref[h : h + 1, :] * a_ref[h, at] * a).astype(bf16) for h in range(HL)]
    n_ref[...] = jnp.swapaxes(jnp.stack(normed), 0, 1)
    qg_ref[...] = jnp.swapaxes(qh_ref[:, at], 0, 1)
    for h in range(HL):
        part = mm_upper(kq_ref[h, at], p_ref[h, at]) + mm(k_ref[h, at], wl_ref[step, h])
        vg_ref[h, at] = part.astype(bf16)


def value_part(kh, pre, kq, wloc, att, grad, gain, sums, order):
    return pl.pallas_call(
        value_kernel,
        grid=(NC,),
        in_specs=[HERE] * 9,
        out_specs=[TOK, TOK, HERE, HERE],
        out_shape=[TOKENS, TOKENS, MAJOR, MARK],
        compiler_params=params(14),
        cost_estimate=cost(2 * T * HL * (C * E + E * E), 20 * MIB),
        name="value_part",
    )(*near(kh, pre, kq, wloc, att, grad, gain, *sums, order))


def final_half(first, l_ref, k_ref, v_ref, kg_ref, vg_ref, at):
    for j in range(HALF):
        h = first + j
        kg_ref[h, at] = (kg_ref[h, at].astype(f32) + mm_nt(v_ref[h, at], l_ref[j])).astype(bf16)
    for j in range(HALF):
        h = first + j
        vg_ref[h, at] = (vg_ref[h, at].astype(f32) + mm(k_ref[h, at], l_ref[j])).astype(bf16)


def in_order(l_ref, x_ref):
    for j in range(HALF):
        parts = []
        for n in range(L * L):
            first = 64 * (n // L) + 8 * j
            parts.append(x_ref[n % L, first : first + 8, :])
        l_ref[j] = jnp.concatenate(parts, axis=0).astype(bf16)


def final_own_kernel(step, mine, other, k_ref, v_ref, own_ref, _, __, kg_ref, vg_ref, l_ref):

    @pl.when(step == 0)
    def _():
        in_order(l_ref, own_ref)

    final_half(mine, l_ref, k_ref, v_ref, kg_ref, vg_ref, rows(step))


def final_own(kh, vh, own, kpart, vpart):
    return pl.pallas_call(
        by_core(by_chunk(final_own_kernel)),
        in_specs=[HERE] * 5,
        out_specs=[HERE] * 2,
        out_shape=[MAJOR] * 2,
        input_output_aliases={3: 0, 4: 1},
        scratch_shapes=[pltpu.VMEM((HALF, E, E), bf16)],
        compiler_params=params(4),
        cost_estimate=cost(2 * T * HL * E * E, 8 * MIB),
        name="final_own",
    )(*near(kh, vh, own, kpart, vpart))


def final_got_kernel(
    mine, other, k_ref, v_ref, got_ref, kp_ref, vp_ref, mine_ref, theirs_ref, kg_ref, vg_ref, e_ref, l_ref
):
    step = pl.program_id(0)
    at = rows(step)

    @pl.when(step == 0)
    def _():
        in_order(l_ref, got_ref)
        e_ref[mine * L : (mine + HALF) * L] = mine_ref[...]
        e_ref[other * L : (other + HALF) * L] = theirs_ref[...]

    final_half(other, l_ref, k_ref, v_ref, kp_ref, vp_ref, at)
    kg_ref[...] = jnp.swapaxes(kp_ref[:, at], 0, 1)
    vg_ref[...] = jnp.swapaxes(vp_ref[:, at], 0, 1)


def final_got(kh, vh, got, kpart, vpart, mine, theirs):
    return pl.pallas_call(
        by_core(final_got_kernel),
        grid=(NC,),
        in_specs=[HERE] * 7,
        out_specs=[TOK] * 2 + [HERE],
        out_shape=[TOKENS] * 2 + [jax.ShapeDtypeStruct((HL * L, E), f32)],
        scratch_shapes=[pltpu.VMEM((HALF, E, E), bf16)],
        compiler_params=params(14),
        cost_estimate=cost(2 * T * HL * E * E, 15 * MIB),
        name="final_got",
    )(*near(kh, vh, got, kpart, vpart, mine, theirs))


def along(x, move):
    def seq(y, z, core):
        return (y * L + z) * 2 + core

    places = [(y, z, core) for y in range(L) for z in range(L) for core in range(2)]
    return lax.ppermute(x, "seq", [(seq(*p), seq(*move(*p))) for p in places])


def across_cores(x):
    return along(x, lambda y, z, core: (y, z, 1 - core))


def across_z(parts):
    return list(parts[:1]) + [
        along(x, lambda y, z, core: (y, (z + k) % L, core)) for x, k in zip(parts[1:], ZSTEPS[1:])
    ]


def across_y(x):
    return [along(x, lambda y, z, core: ((y + k) % L, z, core)) for k in YSTEPS]


def add_kernel(a_ref, b_ref, o_ref):
    o_ref[...] = a_ref[...] + b_ref[...]


def across_heads(x):
    for partner in (lambda i: i ^ 1, lambda i: X - 1 - i):
        got = lax.ppermute(x, "head", [(i, partner(i)) for i in range(X)])
        x = pl.pallas_call(
            add_kernel,
            in_specs=[HERE] * 2,
            out_specs=HERE,
            out_shape=pltpu.VMEM((NC, 2, C), f32),
            compiler_params=params(2),
            name="add",
        )(*near(x, got))
    return [x]


def body(queries, keys, values, out_grad, gain, entry_state):
    rows_of = HALF * E // L
    start = entry_state.reshape(2 * L, rows_of, E)
    kh, vh, other = kv_other(keys, values)
    got = across_cores(other.reshape(L, rows_of, E))
    *parts, extra = pair(kv_mine(kh, vh).reshape(L, rows_of, E), got, 0)
    near_row = across_z(parts)
    qh, loc, start, mark = local_states(queries, kh, vh, start, parts[0])
    inrow, total = row_sums(near_row, mark, False)
    others = across_y(total)
    part, mark = inner_part(qh, kh, vh, loc, total)
    parts = prior_sums(inrow, others, start, mark)
    scan = across_z(parts)
    gh, kq, mark = square_part(out_grad, qh, kh, parts[0])
    own, other = split(scan, extra, mark, 0)
    got = across_cores(other)
    att, state, sums = stats_own(qh, gh, part, own.reshape(HALF, E, E), gain)
    got = got.reshape(HALF, E, E)
    att, state, sums = stats_got(qh, gh, part, got, gain, sums, att, state)
    sums = across_heads(sums)
    pre, wloc, other = pre_part(qh, gh, att, gain, sums)
    got = across_cores(other)
    pre, wloc, mine = pre_part(qh, gh, att, gain, sums, pre, wloc)
    *parts, extra = pair(mine, got, 1)
    near_row = across_z(parts)
    grad, mark = query_part(kh, vh, pre, state, loc, parts[0])
    inrow, total = row_sums(near_row, mark, True)
    others = across_y(total)
    kpart, mark = key_part(qh, vh, pre, wloc, total)
    *parts, mine, theirs = later_sums(inrow, total, others, mark)
    scan = across_z(parts)
    theirs = across_cores(theirs)
    normed, query_grad, vpart, mark = value_part(
        kh, pre, kq, wloc, att, grad, gain, sums, parts[0]
    )
    own, other = split(scan, extra, mark, 1)
    got = across_cores(other)
    kpart, vpart = final_own(kh, vh, own, kpart, vpart)
    key_grad, value_grad, entry_grad = final_got(kh, vh, got, kpart, vpart, mine, theirs)
    return normed, query_grad, key_grad, value_grad, entry_grad.reshape(HL, L, E)


def solution(mesh):
    tok = P("seq", "head", None)
    return jax.shard_map(
        body,
        mesh=mesh,
        in_specs=(tok, tok, tok, tok, P("head", None), P("head", None, None)),
        out_specs=(tok, tok, tok, tok, P("head", "seq", None)),
        check_vma=False,
    )
```
